256 devices in a mesh: row: 4 (over x), col: 32 (over z, y), depth: 2 (over core).
Axes of the slice: x: 4, y: 4, z: 8, core: 2. Of those that a mesh axis runs over, the one named last changes fastest.
Arguments:
- xmat: bfloat16 [8192, 8192], P('row', ('col', 'depth'))
- mask_x: int32 [64, 64], P('row', ('col', 'depth')), may hold values from 0 to 1, as said below
- mask_sq: int32 [64, 64], P('row', ('col', 'depth')), may hold values from 0 to 1, as said below
- mask_out: int32 [64, 64], P('row', ('col', 'depth')), may hold values from 0 to 1, as said below
Outputs:
- new_iterate: bfloat16 [8192, 8192], P('row', ('col', 'depth'))
The draws below stay inside these ranges and needn't reach their ends.
Inputs may be any that keep to these rules, and one draw needn't show every extreme that they name: `mask_x`: 0 or 1 for each block; every diagonal block is 1; in each aligned group of 16 block rows (rows 0 to 15, 16 to 31 and so on) every block column holds at most 4 ones, and block column 0 holds exactly 4 in every group. `mask_sq`: 0 or 1 for each block; every diagonal block is 1. `mask_out`: 0 or 1 for each block; every diagonal block is 1.
All inputs are finite; a program needn't handle non-finite values.
Results may differ from the reference program's by a relative error of at most 0.013.
Values may be sent and summed in bfloat16 or wider, within the bound.
A program may use at most 128 MiB of HBM per device.

```python
import math
import jax
import jax.numpy as jnp
from jax import lax

BS = 128
COLB = 1
NB = 64
N_ROW = 4
N_COL = 32
N_DEPTH = 2


def block_pattern(key, lowest, highest):
    first, second = jax.random.split(key)
    rates = jax.random.randint(first, (NB, 1), lowest, highest)
    picks = jax.random.randint(second, (NB, NB), 0, 256)
    diagonal = jnp.arange(NB)[:, None] == jnp.arange(NB)[None, :]
    return jnp.where(diagonal | (picks < rates), 1, 0).astype(jnp.int32)


def draw_xmat(key, part):
    key = jax.random.fold_in(key, 11)
    order = NB * BS
    first, second, third = jax.random.split(key, 3)
    spread = 0.6 / math.sqrt(BS * (1.0 + 0.09 * NB))
    noise = jax.random.normal(first, (order, order), jnp.float32)
    sizes = jax.random.uniform(second, (order,), jnp.float32, 0.5, 1.2)
    signs = jnp.where(jax.random.bernoulli(third, 0.5, (order,)), 1.0, -1.0)
    index = jnp.arange(order)
    matrix = (noise * spread).at[index, index].add(sizes * signs)
    return matrix.astype(jnp.bfloat16)


def draw_mask_x(key, part):
    key = jax.random.fold_in(key, 21)
    first, second = jax.random.split(key)
    group_rows = NB // N_ROW
    most = min(4, group_rows)
    local = jnp.arange(group_rows, dtype=jnp.int32)
    scores = jax.random.randint(first, (N_ROW, group_rows, NB), 0, 1024) * group_rows + local[None, :, None]
    global_row = jnp.arange(N_ROW, dtype=jnp.int32)[:, None, None] * group_rows + local[None, :, None]
    column = jnp.arange(NB, dtype=jnp.int32)[None, None, :]
    scores = jnp.where(global_row == column, 1024 * group_rows * 2, scores)
    order = jnp.argsort(-scores, axis=1)
    ranks = jnp.argsort(order, axis=1)
    counts = jax.random.randint(second, (N_ROW, 1, NB), 1, most + 1)
    counts = counts.at[:, :, 0].set(most)
    kept = ranks < counts
    return jnp.where(kept, 1, 0).astype(jnp.int32).reshape(NB, NB)


def draw_mask_sq(key, part):
    key = jax.random.fold_in(key, 22)
    return block_pattern(key, 40, 200)


def draw_mask_out(key, part):
    key = jax.random.fold_in(key, 23)
    return block_pattern(key, 20, 120)


def setup_inputs(seed: int = 0) -> dict:
    keys = jax.random.split(jax.random.key(seed), 5)
    xmat = draw_xmat(jax.random.fold_in(keys[4], 71), 0)
    mask_x = draw_mask_x(jax.random.fold_in(keys[4], 71), 0)
    mask_sq = draw_mask_sq(jax.random.fold_in(keys[4], 71), 0)
    mask_out = draw_mask_out(jax.random.fold_in(keys[4], 71), 0)
    return dict(xmat=xmat, mask_x=mask_x, mask_sq=mask_sq, mask_out=mask_out)


def masked(values, pattern):
    rows, cols = pattern.shape
    block = values.shape[0] // rows
    shaped = values.reshape(rows, block, cols, block)
    keep = pattern[:, None, :, None].astype(values.dtype)
    return (shaped * keep).reshape(values.shape)


def layered_product(left, right):
    order = left.shape[0]
    left_split = left.reshape(order, N_COL, N_DEPTH, COLB * BS)
    right_split = right.reshape(N_COL, N_DEPTH, COLB * BS, order)
    total = jnp.zeros((order, order), jnp.float32)
    for layer in range(N_DEPTH):
        left_part = left_split[:, :, layer, :].reshape(order, N_COL * COLB * BS)
        right_part = right_split[:, layer].reshape(N_COL * COLB * BS, order)
        term = jnp.dot(left_part, right_part, preferred_element_type=jnp.float32).astype(jnp.bfloat16)
        term = lax.optimization_barrier(term)
        total = total + term.astype(jnp.float32)
    return total


def reference(xmat, mask_x, mask_sq, mask_out):
    xmask = masked(xmat, mask_x)
    square = masked(layered_product(xmask, xmask), mask_sq).astype(jnp.bfloat16)
    cube = layered_product(xmask, square)
    result = 1.5 * xmask.astype(jnp.float32) - 0.5 * cube
    return masked(result, mask_out).astype(jnp.bfloat16)
```

```python
import jax
import jax.numpy as jnp
from jax import lax
from jax.experimental import pallas as pl
from jax.experimental.pallas import tpu as pltpu
from jax.sharding import PartitionSpec as P

BS = 128
RB = 16
SLOTS = 4
NX, NY, NZ = 4, 4, 8
NC = NY * NZ
HALF = BS // 2
RA = 3 * HALF
RZ = SLOTS * BS - RA
B0 = 2 * NC * RA
ZERO = B0 + 2 * NC * RZ
ROWS = RB * BS
QR = 4
QN = RB // QR
MSGS = 128

UP = (0, -1, 2, -3)


def a_off(core, z, y):
    return pl.multiple_of(((core * NZ + z) * NY + y) * RA, HALF)


def b_off(core, y, z):
    return pl.multiple_of(B0 + ((core * NY + y) * NZ + z) * RZ, HALF)


def kernel(mx, msq, mo, x_ref, out_ref, panel, xc, sb, acc, at_v, ct_v, at_s, ct_s,
           send_sem, recv_sem, local_sem):
    x = lax.axis_index("row")
    c = lax.axis_index("col")
    d = lax.axis_index("depth")
    z, y = c // NY, c % NY
    e = 1 - d

    def yy(k):
        return (y + (k + NY)) % NY

    def zz(k):
        return (z + (k + NZ)) % NZ

    def xx(k):
        return (x + (k + NX)) % NX

    def dev(dx=0, dy=0, dz=0, core=None):
        return {
            "row": xx(dx) if dx else x,
            "col": (zz(dz) if dz else z) * NY + (yy(dy) if dy else y),
            "depth": d if core is None else core,
        }

    yp, ym, zp, zm = dev(dy=1), dev(dy=-1), dev(dz=1), dev(dz=-1)
    xp, xm, x2, sib = dev(dx=1), dev(dx=-1), dev(dx=2), dev(core=e)
    partners = (yp, ym, zp, zm, xp, xm, x2, sib)

    barrier = pltpu.get_barrier_semaphore()
    for partner in partners:
        pl.semaphore_signal(
            barrier, inc=1, device_id=partner, device_id_type=pl.DeviceIdType.MESH
        )

    count = jnp.int32(0)
    index = [jnp.int32(0)] * SLOTS
    lane = lax.broadcasted_iota(jnp.int32, (1, 128), 1)
    abase = a_off(d, z, y) // HALF
    bbase = b_off(d, y, z) // HALF
    entry = jnp.full((1, 128), ZERO // HALF, jnp.int32)
    for i in range(RB):
        keep = jnp.minimum(mx[i], 1)
        for s in range(SLOTS):
            here = jnp.maximum(1 - jnp.abs(count - s), 0)
            index[s] = index[s] + i * keep * here
        for h in range(2):
            g = 2 * count + h
            low = jnp.minimum(jnp.maximum(3 - g, 0), 1)
            at = low * (abase + g) + (1 - low) * (bbase + g - 3)
            at = keep * at + (1 - keep) * (ZERO // HALF)
            entry = jnp.where(lane == 2 * i + h, at, entry)
        count = count + keep
    column = jnp.full((1, 128), 2 * NC, jnp.int32)
    for s in range(SLOTS):
        there = jnp.minimum(jnp.maximum(count - s, 0), 1)
        k = there * (x * RB + index[s]) + (1 - there) * (2 * NC)
        column = jnp.where(lane == s, k, column)
    at_v[2 * c + d] = entry
    for core in range(2):
        at_v[2 * NC + core] = jnp.full((1, 128), ZERO // HALF, jnp.int32)
    ct_v[x] = column
    panel[pl.ds(ZERO, HALF)] = jnp.zeros((HALF, BS), jnp.bfloat16)
    for s in range(SLOTS):
        for h in range(2):
            g = 2 * s + h
            piece = x_ref[pl.ds(index[s] * BS + h * HALF, HALF)]
            base = a_off(d, z, y) + HALF * g if g < 3 else b_off(d, y, z) + HALF * (g - 3)
            panel[pl.ds(pl.multiple_of(base, HALF), HALF)] = piece
            xc[pl.ds(pl.multiple_of(x * (SLOTS * BS) + g * HALF, HALF), HALF)] = piece

    pl.semaphore_wait(barrier, len(partners))

    names = {}
    sent = []

    def copy(name, src, dst, target):
        m = names.setdefault(name, len(names))
        return pltpu.make_async_remote_copy(
            src_ref=src, dst_ref=dst, send_sem=send_sem.at[m], recv_sem=recv_sem.at[m],
            device_id=target, device_id_type=pl.DeviceIdType.MESH,
        )

    def send(name, ref, target):
        made = copy(name, ref, ref, target)
        made.start()
        sent.append(made)

    def recv(name, ref, target):
        copy(name, ref, ref, target).wait_recv()

    def pa(core, z_, y_, first=0, rows=RA):
        return panel.at[pl.ds(pl.multiple_of(a_off(core, z_, y_) + first, 16), rows)]

    def pb(core, y_, z_, first=0, rows=RZ):
        return panel.at[pl.ds(pl.multiple_of(b_off(core, y_, z_) + first, 16), rows)]

    late = []

    def share(name, ref_of):
        send("s" + name, ref_of(d), sib)
        late.append(("s" + name, ref_of(e)))

    def b_chunk(k):
        send(f"by+{k}", pb(d, y, zz(k)), yp)
        send(f"by-{k}", pb(d, y, zz(k)), ym)
        share(f"b0{k}", lambda core: pb(core, y, zz(k)))

    def b_arrive(k):
        recv(f"by+{k}", pb(d, yy(-1), zz(k)), yp)
        if k in UP:
            send(f"bf{k}", pb(d, yy(-1), zz(k)), yp)
        recv(f"by-{k}", pb(d, yy(1), zz(k)), ym)
        if k not in UP:
            send(f"bf{k}", pb(d, yy(1), zz(k)), ym)
        share(f"b-{k}", lambda core: pb(core, yy(-1), zz(k)))
        share(f"b+{k}", lambda core: pb(core, yy(1), zz(k)))

    def b_last(k):
        recv(f"bf{k}", pb(d, yy(2), zz(k)), yp if k in UP else ym)
        share(f"b2{k}", lambda core: pb(core, yy(2), zz(k)))

    def entries(y_):
        return at_v.at[pl.ds(pl.multiple_of((z * NY + y_) * 2, 2), 2)]

    def table(z_):
        return at_v.at[pl.ds(pl.multiple_of(z_ * (2 * NY), 2), 2 * NY)]

    group = NY * RA

    def a_group(s):
        if s < 3:
            send(f"az+{s}", pa(d, zz(-s), 0, 0, group), zp)
            send(f"az-{s}", pa(d, zz(s), 0, 0, group), zm)
            send(f"tz-{s}", table(zz(s)), zm)
        else:
            send(f"az+{s}", pa(d, zz(-s), 0, 0, group // 2), zp)
            send(f"az-{s}", pa(d, zz(s), 0, group // 2, group // 2), zm)
        send(f"tz+{s}", table(zz(-s)), zp)

    def a_arrive(s):
        k = s + 1
        if s < 3:
            recv(f"az+{s}", pa(d, zz(-k), 0, 0, group), zp)
            recv(f"az-{s}", pa(d, zz(k), 0, 0, group), zm)
            recv(f"tz-{s}", table(zz(k)), zm)
            recv(f"tz+{s}", table(zz(-k)), zp)
            a_group(k)
            share(f"a-{k}", lambda core: pa(core, zz(-k), 0, 0, group))
            share(f"a+{k}", lambda core: pa(core, zz(k), 0, 0, group))
        else:
            recv(f"az+{s}", pa(d, zz(4), 0, 0, group // 2), zp)
            recv(f"az-{s}", pa(d, zz(4), 0, group // 2, group // 2), zm)
            recv(f"tz+{s}", table(zz(4)), zp)
            share("a4", lambda core: pa(core, zz(4), 0, 0, group))

    send("t0", at_v.at[2 * c + d], sib)
    send("ay+", pa(d, z, y), yp)
    send("ay-", pa(d, z, y), ym)
    send("bz+0", pb(d, y, z), zp)
    send("bz-0", pb(d, y, z), zm)
    share("a0", lambda core: pa(core, z, y))
    b_chunk(0)
    own = xc.at[pl.ds(pl.multiple_of(x * (SLOTS * BS), BS), SLOTS * BS)]
    for name, target in (("x+", xp), ("x-", xm), ("x2", x2)):
        send("c" + name, ct_v.at[x], target)
        send(name, own, target)
    recv("t0", at_v.at[2 * c + e], sib)
    send("ty+", entries(y), yp)
    send("ty-", entries(y), ym)

    recv("ay+", pa(d, z, yy(-1)), yp)
    send("af+", pa(d, z, yy(-1), 0, RA // 2), yp)
    recv("ay-", pa(d, z, yy(1)), ym)
    send("af-", pa(d, z, yy(1), RA // 2, RA // 2), ym)
    share("ay-", lambda core: pa(core, z, yy(-1)))
    share("ay+", lambda core: pa(core, z, yy(1)))
    recv("ty+", entries(yy(-1)), yp)
    send("tf", entries(yy(-1)), yp)
    recv("ty-", entries(yy(1)), ym)

    def bz_arrive(s):
        k = s + 1
        if s < 3:
            recv(f"bz+{s}", pb(d, y, zz(-k)), zp)
            recv(f"bz-{s}", pb(d, y, zz(k)), zm)
            if k < 3:
                send(f"bz+{k}", pb(d, y, zz(-k)), zp)
                send(f"bz-{k}", pb(d, y, zz(k)), zm)
            else:
                send(f"bz+{k}", pb(d, y, zz(-k), 0, RZ // 2), zp)
                send(f"bz-{k}", pb(d, y, zz(k), RZ // 2, RZ // 2), zm)
            b_chunk(-k)
            b_chunk(k)
        else:
            recv(f"bz+{s}", pb(d, y, zz(4), 0, RZ // 2), zp)
            recv(f"bz-{s}", pb(d, y, zz(4), RZ // 2, RZ // 2), zm)
            b_chunk(4)

    bz_arrive(0)
    recv("af+", pa(d, z, yy(2), 0, RA // 2), yp)
    recv("af-", pa(d, z, yy(2), RA // 2, RA // 2), ym)
    recv("tf", entries(yy(2)), yp)
    a_group(0)
    share("ay2", lambda core: pa(core, z, yy(2)))
    bz_arrive(1)
    b_arrive(0)
    bz_arrive(2)
    b_arrive(-1)
    b_arrive(1)
    bz_arrive(3)
    a_arrive(0)
    b_arrive(-2)
    b_arrive(2)
    a_arrive(1)
    b_arrive(-3)
    b_arrive(3)
    b_arrive(4)
    a_arrive(2)
    for k in (0, 1, -1, -2, 2, 3, -3, 4):
        b_last(k)
    a_arrive(3)
    for name, k, target in (("x+", -1, xp), ("x-", 1, xm), ("x2", 2, x2)):
        recv("c" + name, ct_v.at[xx(k)], target)
        recv(name, xc.at[pl.ds(pl.multiple_of(xx(k) * (SLOTS * BS), BS), SLOTS * BS)], target)
    tables = [
        pltpu.make_async_copy(at_v, at_s, local_sem.at[0]),
        pltpu.make_async_copy(ct_v, ct_s, local_sem.at[1]),
    ]
    for made in tables:
        made.start()
    for name, ref in late:
        recv(name, ref, sib)
    for made in tables:
        made.wait()

    def block(k, i):
        halves = [panel[pl.ds(at_s[k, 0, 2 * i + h] * HALF, HALF)] for h in range(2)]
        return jnp.concatenate(halves, axis=0)

    def tile(rows, columns):
        return jnp.concatenate(
            [jnp.concatenate([block(k, i) for k in columns], axis=1) for i in rows], axis=0
        )

    def masked(flag, values):
        return jnp.where(jnp.full(values.shape, flag, jnp.int32) != 0, values, 0.0)

    def s_ref(group_, first, rows):
        return sb.at[pl.ds(pl.multiple_of(group_ * ROWS + first, 16), rows)]

    qrows = QR * BS
    for q in range(QN):
        rows = [q * QR + i for i in range(QR)]

        def pair(p, carry):
            columns = [ct_s[p // 2, 0, (p % 2) * 2 + j] for j in range(2)]
            term = jnp.dot(
                tile(rows, columns),
                xc[pl.ds(pl.multiple_of(p * 2 * BS, BS), 2 * BS)],
                preferred_element_type=jnp.float32,
            )
            here = pl.ds(0, qrows)
            acc[here] = jnp.where(p == 0, term, acc[here] + term)
            return carry

        lax.fori_loop(0, NX * SLOTS // 2, pair, 0)
        for i in range(QR):
            part = masked(msq[q * QR + i], acc[pl.ds(i * BS, BS)])
            first = pl.multiple_of(x * ROWS + (q * QR + i) * BS, BS)
            sb[pl.ds(first, BS)] = part.astype(jnp.bfloat16)
        send(f"q+{q}", s_ref(x, q * qrows, qrows), xp)
        send(f"q-{q}", s_ref(x, q * qrows, qrows), xm)

    acc[...] = jnp.zeros_like(acc)

    def cube(group_, q):
        w = sb[pl.ds(pl.multiple_of(group_ * ROWS + q * qrows, BS), qrows)]
        columns = [group_ * RB + q * QR + k for k in range(QR)]

        def rows4(ig, carry):
            here = pl.ds(pl.multiple_of(ig * qrows, BS), qrows)
            acc[here] += jnp.dot(
                tile([ig * QR + i for i in range(QR)], columns), w,
                preferred_element_type=jnp.float32,
            )
            return carry

        lax.fori_loop(0, RB // QR, rows4, 0)

    def s_arrive(q):
        recv(f"q+{q}", s_ref(xx(-1), q * qrows, qrows), xp)
        send(f"f+{q}", s_ref(xx(-1), q * qrows, qrows // 2), xp)
        recv(f"q-{q}", s_ref(xx(1), q * qrows, qrows), xm)
        send(f"f-{q}", s_ref(xx(1), q * qrows + qrows // 2, qrows // 2), xm)

    def s_last(q):
        recv(f"f+{q}", s_ref(xx(2), q * qrows, qrows // 2), xp)
        recv(f"f-{q}", s_ref(xx(2), q * qrows + qrows // 2, qrows // 2), xm)

    cube(x, 0)
    cube(x, 1)
    s_arrive(0)
    cube(x, 2)
    cube(x, 3)
    s_arrive(1)
    cube(xx(-1), 0)
    cube(xx(1), 0)
    s_arrive(2)
    cube(xx(-1), 1)
    cube(xx(1), 1)
    s_last(0)
    cube(xx(2), 0)
    s_arrive(3)
    cube(xx(-1), 2)
    cube(xx(1), 2)
    s_last(1)
    cube(xx(2), 1)
    cube(xx(-1), 3)
    cube(xx(1), 3)
    s_last(2)
    cube(xx(2), 2)
    s_last(3)
    cube(xx(2), 3)

    for i in range(RB):
        here = pl.ds(i * BS, BS)
        kept = masked(mx[i], x_ref[here].astype(jnp.float32))
        result = masked(mo[i], 1.5 * kept - 0.5 * acc[here])
        out_ref[here] = result.astype(jnp.bfloat16)

    for made in sent:
        made.wait_send()


def body(xmat, mask_x, mask_sq, mask_out):
    smem = pl.BlockSpec(memory_space=pltpu.SMEM)
    vmem = pl.BlockSpec(memory_space=pltpu.VMEM)
    return pl.pallas_call(
        kernel,
        out_shape=jax.ShapeDtypeStruct(xmat.shape, jnp.bfloat16),
        in_specs=[smem, smem, smem, vmem],
        out_specs=vmem,
        scratch_shapes=[
            pltpu.VMEM((ZERO + HALF, BS), jnp.bfloat16),
            pltpu.VMEM((NX * SLOTS * BS, BS), jnp.bfloat16),
            pltpu.VMEM((NX * ROWS, BS), jnp.bfloat16),
            pltpu.VMEM((ROWS, BS), jnp.float32),
            pltpu.VMEM((2 * NC + 2, 1, 128), jnp.int32),
            pltpu.VMEM((NX, 1, 128), jnp.int32),
            pltpu.SMEM((2 * NC + 2, 1, 128), jnp.int32),
            pltpu.SMEM((NX, 1, 128), jnp.int32),
            pltpu.SemaphoreType.DMA((MSGS,)),
            pltpu.SemaphoreType.DMA((MSGS,)),
            pltpu.SemaphoreType.DMA((2,)),
        ],
        compiler_params=pltpu.CompilerParams(
            collective_id=0, has_side_effects=True, vmem_limit_bytes=48 * 1024 * 1024
        ),
    )(mask_x.reshape(RB), mask_sq.reshape(RB), mask_out.reshape(RB), xmat)


def solution(mesh):
    placed = P("row", ("col", "depth"))
    return jax.shard_map(
        body, mesh=mesh, in_specs=(placed,) * 4, out_specs=placed, check_vma=False
    )
```

```python
import jax
import jax.numpy as jnp
from jax import lax
from jax.experimental import pallas as pl
from jax.experimental.pallas import tpu as pltpu
from jax.sharding import PartitionSpec as P

BS = 128
RB = 16
SLOTS = 4
NX, NY, NZ = 4, 4, 8
NC = NY * NZ
HALF = BS // 2
RA = 192
RZ = SLOTS * BS - RA
B0 = 2 * NC * RA
ZERO = B0 + 2 * NC * RZ
ROWS = RB * BS
QS = (0, 2, 6, 10, 14)
QL = (2, 4, 4, 4, 2)
TILES = ((0, 2), (2, 4), (6, 8), (14, 2))
TR = 8
MSGS = 144

PARTS = ((0, 96), (96, 96), (0, 160), (160, 160))

ORDER = (
    -4, -52, -107, -77, -68, -116, -75, -45, -36, -84, -109, -43, -100, -20, -11, -13, 3, 51,
    -28, -60, -3, -5, 106, 76, -99, -85, -106, -78, 67, 115, 44, 74, -67, -83, -74, -124, 35,
    -37, 83, 108, 42, -110, -101, -69, -117, -92, -115, 99, 19, 10, 12, -19, -35, -14, -21, 128,
    27, 59, 2, 4, -27, -59, -29, 98, 84, 105, 77, -105, -79, -70, -86, 36, -38, 66, 82, 73, -73,
    -82, 109, 18, -102, -111, -18, -66, -118, 100, 123, 34, 13, -15, 26, 20, -26, 68, 116, -93,
    -125, 58, 28, -58, -30, -42, -61, -10, -53, -2, 91, 114, -123, 104, 78, -71, -97, -113,
    -114, -87, 69, 85, 37, -39, -46, 72, -80, 101, 81, 110, 17, -112, -103, -94, -119, -81, 129,
    25, 14, -25, -51, 65, 117, -90, 57, 29, -31, 41, 60, -41, -62, 92, 124, 9, 52, -9, -54, -6,
    1, 38, 70, 122, -1, -95, -34, -57, 45, -47, -40, -22, 96, 112, 79, -72, -65, 111, 24, -120,
    -32, -104, -98, -91, 102, 113, -122, -121, 50, 30, -50, -17, 40, 61, -63, 93, 86, 8, 53,
    -55, -16, 0, 5, 89, 118, -7, -8, -127, -126, 33, 46, -48, -33, 130, 94, 80, 56, 39, 31, 21,
    -23, 71, 119, -96, -128, -88, 49, -49, 62, -64, 64, 121, 16, -24, -89, 54, -56, 15, 6, 103,
    120, 7, 47, 32, 97, 126, 22, 90, 125, 48, 63, 23, 55, 95, 127, 88, 87,
)


def a_off(core, z, y):
    return pl.multiple_of(((core * NZ + z) * NY + y) * RA, HALF)


def b_off(core, y, z):
    return pl.multiple_of(B0 + ((core * NY + y) * NZ + z) * RZ, HALF)


def kernel(mx_hbm, msq_hbm, mo_hbm, x_hbm, out_ref, mx, msq, mo, x_ref, panel, xc, sb, acc,
           at_v, ct_v, at_s, ct_s, send_sem, recv_sem, local_sem):
    x = lax.axis_index("row")
    c = lax.axis_index("col")
    d = lax.axis_index("depth")
    z, y = c // NY, c % NY
    e = 1 - d

    def yy(k):
        return (y + (k + NY)) % NY

    def zz(k):
        return (z + (k + NZ)) % NZ

    def xx(k):
        return (x + (k + NX)) % NX

    def dev(dx=0, dy=0, dz=0, core=None):
        return {
            "row": xx(dx) if dx else x,
            "col": (zz(dz) if dz else z) * NY + (yy(dy) if dy else y),
            "depth": d if core is None else core,
        }

    yp, ym, zp, zm = dev(dy=1), dev(dy=-1), dev(dz=1), dev(dz=-1)
    xp, xm, x2, sib = dev(dx=1), dev(dx=-1), dev(dx=2), dev(core=e)
    y2, zpp, zmm = dev(dy=2), dev(dz=2), dev(dz=-2)
    partners = (zp, zm, yp, ym, zpp, zmm, y2, xp, xm, x2, sib)

    barrier = pltpu.get_barrier_semaphore()
    for partner in partners:
        pl.semaphore_signal(
            barrier, inc=1, device_id=partner, device_id_type=pl.DeviceIdType.MESH
        )

    inputs = [
        pltpu.make_async_copy(src, dst, local_sem.at[2 + n])
        for n, (src, dst) in enumerate(
            ((mx_hbm, mx), (msq_hbm, msq), (mo_hbm, mo), (x_hbm, x_ref))
        )
    ]
    for made in inputs:
        made.start()
    panel[pl.ds(ZERO, HALF)] = jnp.zeros((HALF, BS), jnp.bfloat16)
    for made in inputs:
        made.wait()

    count = jnp.int32(0)
    index = [jnp.int32(0)] * SLOTS
    lane = lax.broadcasted_iota(jnp.int32, (1, 128), 1)
    abase = a_off(d, z, y) // HALF
    bbase = b_off(d, y, z) // HALF
    entry = jnp.full((1, 128), ZERO // HALF, jnp.int32)
    for i in range(RB):
        keep = jnp.minimum(mx[i], 1)
        for s in range(SLOTS):
            here = jnp.maximum(1 - jnp.abs(count - s), 0)
            index[s] = index[s] + i * keep * here
        for h in range(2):
            g = 2 * count + h
            low = jnp.minimum(jnp.maximum(3 - g, 0), 1)
            at = low * (abase + g) + (1 - low) * (bbase + g - 3)
            at = keep * at + (1 - keep) * (ZERO // HALF)
            entry = jnp.where(lane == 2 * i + h, at, entry)
        count = count + keep
    column = jnp.full((1, 128), 2 * NC, jnp.int32)
    for s in range(SLOTS):
        there = jnp.minimum(jnp.maximum(count - s, 0), 1)
        k = there * (x * RB + index[s]) + (1 - there) * (2 * NC)
        column = jnp.where(lane == s, k, column)
    at_v[2 * c + d] = entry
    for core in range(2):
        at_v[2 * NC + core] = jnp.full((1, 128), ZERO // HALF, jnp.int32)
    ct_v[x] = column
    for s in range(SLOTS):
        for h in range(2):
            g = 2 * s + h
            piece = x_ref[pl.ds(index[s] * BS + h * HALF, HALF)]
            base = a_off(d, z, y) + HALF * g if g < 3 else b_off(d, y, z) + HALF * (g - 3)
            panel[pl.ds(pl.multiple_of(base, HALF), HALF)] = piece
            xc[pl.ds(pl.multiple_of(x * (SLOTS * BS) + g * HALF, HALF), HALF)] = piece

    pl.semaphore_wait(barrier, len(partners))

    names = {}
    sent = {}
    together = {"s": "s", "x": "x", "c": "c", "ty": "ty", "tz": "tz", "t3": "t3", "t4": "t3"}

    def copy(name, src, dst, target):
        key = together.get(name[0], together.get(name[:2], name))
        if name[0] in "qf":
            key = name[0] + name[2:]
        m = names.setdefault(key, len(names))
        kind = {"s": 1, "q": 2, "f": 2, "t": 3, "c": 3}.get(name[0], 0)
        made = pltpu.make_async_remote_copy(
            src_ref=src, dst_ref=dst, send_sem=send_sem.at[kind], recv_sem=recv_sem.at[m],
            device_id=target, device_id_type=pl.DeviceIdType.MESH,
        )
        return made, kind

    def send(name, ref, target):
        made, kind = copy(name, ref, ref, target)
        made.start()
        sent[kind] = sent.get(kind, 0) + ref.shape[0]

    def recv(name, ref, target):
        copy(name, ref, ref, target)[0].wait_recv()

    def pa(core, z_, y_, first=0, rows=RA):
        return panel.at[pl.ds(pl.multiple_of(a_off(core, z_, y_) + first, 16), rows)]

    def pb(core, y_, z_, first=0, rows=RZ):
        return panel.at[pl.ds(pl.multiple_of(b_off(core, y_, z_) + first, 16), rows)]

    def share(name, ref_of):
        send("s" + name, ref_of(d), sib)

    def entries(y_):
        return at_v.at[pl.ds(pl.multiple_of((z * NY + y_) * 2, 2), 2)]

    def table(z_):
        return at_v.at[pl.ds(pl.multiple_of(z_ * (2 * NY), 2), 2 * NY)]

    def chunk(part, v, k, core=None):
        core = d if core is None else core
        first, rows = PARTS[part]
        if part < 2:
            return pa(core, zz(k), yy(v), first, rows)
        return pb(core, yy(v), zz(k), first, rows)

    def step_of(part, v, k):
        far = part % 2
        if (k != 0) if part < 2 else (v == 0):
            if k < 0 or (k == 4 and not far):
                return (v, k + 1 if k < 0 else -3), zp
            return (v, k - 1), zm
        if v < 0 or (v == 2 and not far):
            return (v + 1 if v < 0 else -1, k), yp
        return (v - 1, k), ym

    def name_of(part, v, k):
        return f"{part},{v},{k}"

    def send_chunk(part, v, k):
        (pv, pk), target = step_of(part, v, k)
        send(name_of(part, v, k), chunk(part, pv, pk), target)

    def recv_chunk(part, v, k):
        recv(name_of(part, v, k), chunk(part, v, k), step_of(part, v, k)[1])
        arrived(part, v, k)

    here = {}

    def arrived(part, v, k):
        group = (part // 2, v, k)
        here[group] = here.get(group, 0) + 1
        if here[group] == 2 and part < 2:
            share(f"a{v},{k}", lambda core: pa(core, zz(k), yy(v)))
        elif here[group] == 2:
            share(f"b{v},{k}", lambda core: pb(core, yy(v), zz(k)))

    for part in range(4):
        arrived(part, 0, 0)
    send("t0", at_v.at[2 * c + d], sib)
    own = xc.at[pl.ds(pl.multiple_of(x * (SLOTS * BS), BS), SLOTS * BS)]
    for name, target in (("x+", xp), ("x-", xm), ("x2", x2)):
        send("c" + name, ct_v.at[x], target)
        send(name, own, target)
    started = False
    for n in ORDER:
        if n < 128:
            m = n if n >= 0 else -1 - n
            place = (m // 32, m // 8 % 4 - 1, m % 8 - 3)
            if n >= 0 and not started:
                started = True
                recv("t0", at_v.at[2 * c + e], sib)
                for name, target in (("ty+", yp), ("ty-", ym), ("ty2", y2)):
                    send(name, entries(y), target)
            if n >= 0:
                recv_chunk(*place)
            else:
                send_chunk(*place)
        elif n == 128:
            recv("ty", at_v.at[pl.ds(0, 3 * 2)], yp)
            for name, target in (("tz+", zp), ("tz-", zm), ("tzz+", zpp), ("tzz-", zmm)):
                send(name, table(z), target)
        elif n == 129:
            recv("tz", at_v.at[pl.ds(0, 4 * 2 * NY)], zp)
            send("t3+", table(zz(-1)), zpp)
            send("t3-", table(zz(1)), zmm)
            send("t4", table(zz(-2)), zpp)
        else:
            recv("t3", at_v.at[pl.ds(0, 3 * 2 * NY)], zpp)
    recv("c", ct_v.at[pl.ds(0, 3)], xp)
    recv("x", xc.at[pl.ds(0, 3 * SLOTS * BS)], xp)
    tables = [
        pltpu.make_async_copy(at_v, at_s, local_sem.at[0]),
        pltpu.make_async_copy(ct_v, ct_s, local_sem.at[1]),
    ]
    for made in tables:
        made.start()
    recv("s", panel.at[pl.ds(0, NC * SLOTS * BS)], sib)
    for made in tables:
        made.wait()

    def block(k, i):
        halves = [panel[pl.ds(at_s[k, 0, 2 * i + h] * HALF, HALF)] for h in range(2)]
        return jnp.concatenate(halves, axis=0)

    def tile(rows, columns):
        return jnp.concatenate(
            [jnp.concatenate([block(k, i) for k in columns], axis=1) for i in rows], axis=0
        )

    def masked(flag, values):
        return jnp.where(jnp.full(values.shape, flag, jnp.int32) != 0, values, 0.0)

    def s_ref(group_, q, half=None):
        first, rows = QS[q] * BS, QL[q] * BS
        if half is not None:
            rows //= 2
            first += half * rows
        return sb.at[pl.ds(pl.multiple_of(group_ * ROWS + first, BS), rows)]

    for first, count in TILES:
        rows = [first + i for i in range(count)]

        def pair(p, carry):
            columns = [ct_s[p // 2, 0, (p % 2) * 2 + j] for j in range(2)]
            term = jnp.dot(
                tile(rows, columns),
                xc[pl.ds(pl.multiple_of(p * 2 * BS, BS), 2 * BS)],
                preferred_element_type=jnp.float32,
            )
            spot = pl.ds(0, count * BS)
            acc[spot] = jnp.where(p == 0, term, acc[spot] + term)
            return carry

        lax.fori_loop(0, NX * SLOTS // 2, pair, 0)
        for i, row in enumerate(rows):
            part = masked(msq[row], acc[pl.ds(i * BS, BS)])
            sb[pl.ds(pl.multiple_of(x * ROWS + row * BS, BS), BS)] = part.astype(jnp.bfloat16)
        for q in range(len(QS)):
            if first <= QS[q] < first + count:
                send(f"q+{q}", s_ref(x, q), xp)
                send(f"q-{q}", s_ref(x, q), xm)

    acc[...] = jnp.zeros_like(acc)

    def cube(group_, first, count):
        w = sb[pl.ds(pl.multiple_of(group_ * ROWS + first * BS, BS), count * BS)]
        columns = [group_ * RB + first + k for k in range(count)]

        def some(ig, carry):
            spot = pl.ds(pl.multiple_of(ig * (TR * BS), BS), TR * BS)
            acc[spot] += jnp.dot(
                tile([ig * TR + i for i in range(TR)], columns), w,
                preferred_element_type=jnp.float32,
            )
            return carry

        lax.fori_loop(0, RB // TR, some, 0)

    def s_arrive(q):
        recv(f"q+{q}", sb.at[pl.ds(0, 2 * QL[q] * BS)], xp)
        send(f"f+{q}", s_ref(xx(-1), q, 0), xp)
        send(f"f-{q}", s_ref(xx(1), q, 1), xm)

    def s_last(q):
        recv(f"f+{q}", sb.at[pl.ds(0, QL[q] * BS)], xp)
        cube(xx(2), QS[q], QL[q])

    for q in range(len(QS)):
        cube(x, QS[q], QL[q])
    for q in range(len(QS)):
        s_arrive(q)
        if q < len(QS) - 2:
            cube(xx(-1), QS[q], QL[q])
            cube(xx(1), QS[q], QL[q])
    for k in (-1, 1):
        cube(xx(k), QS[-2], QL[-2] + QL[-1])
    for q in range(len(QS)):
        s_last(q)

    for i in range(RB):
        spot = pl.ds(i * BS, BS)
        kept = masked(mx[i], x_ref[spot].astype(jnp.float32))
        result = masked(mo[i], 1.5 * kept - 0.5 * acc[spot])
        out_ref[spot] = result.astype(jnp.bfloat16)

    for kind, buffer in ((0, panel), (1, panel), (2, sb), (3, at_v)):
        if kind in sent:
            whole = buffer.at[pl.ds(0, sent[kind])]
            pltpu.make_async_remote_copy(
                src_ref=whole, dst_ref=whole, send_sem=send_sem.at[kind], recv_sem=recv_sem.at[0],
                device_id=xp, device_id_type=pl.DeviceIdType.MESH,
            ).wait_send()


def body(xmat, mask_x, mask_sq, mask_out):
    hbm = pl.BlockSpec(memory_space=pltpu.HBM)
    vmem = pl.BlockSpec(memory_space=pltpu.VMEM)
    return pl.pallas_call(
        kernel,
        out_shape=jax.ShapeDtypeStruct(xmat.shape, jnp.bfloat16),
        in_specs=[hbm] * 4,
        out_specs=vmem,
        scratch_shapes=[
            pltpu.SMEM((RB,), jnp.int32),
            pltpu.SMEM((RB,), jnp.int32),
            pltpu.SMEM((RB,), jnp.int32),
            pltpu.VMEM((ROWS, BS), jnp.bfloat16),
            pltpu.VMEM((ZERO + HALF, BS), jnp.bfloat16),
            pltpu.VMEM((NX * SLOTS * BS, BS), jnp.bfloat16),
            pltpu.VMEM((NX * ROWS, BS), jnp.bfloat16),
            pltpu.VMEM((ROWS, BS), jnp.float32),
            pltpu.VMEM((2 * NC + 2, 1, 128), jnp.int32),
            pltpu.VMEM((NX, 1, 128), jnp.int32),
            pltpu.SMEM((2 * NC + 2, 1, 128), jnp.int32),
            pltpu.SMEM((NX, 1, 128), jnp.int32),
            pltpu.SemaphoreType.DMA((4,)),
            pltpu.SemaphoreType.DMA((MSGS,)),
            pltpu.SemaphoreType.DMA((6,)),
        ],
        compiler_params=pltpu.CompilerParams(
            collective_id=0, has_side_effects=True, vmem_limit_bytes=60 * 1024 * 1024
        ),
    )(mask_x.reshape(RB), mask_sq.reshape(RB), mask_out.reshape(RB), xmat)


def solution(mesh):
    placed = P("row", ("col", "depth"))
    return jax.shard_map(
        body, mesh=mesh, in_specs=(placed,) * 4, out_specs=placed, check_vma=False
    )
```

```python
import jax
import jax.numpy as jnp
from jax import lax
from jax.experimental import pallas as pl
from jax.experimental.pallas import tpu as pltpu
from jax.sharding import PartitionSpec as P

BS = 128
RB = 16
SLOTS = 4
NX, NY, NZ = 4, 4, 8
NC = NY * NZ
PACK = SLOTS * BS
ZERO = 2 * NC * PACK
ROWS = RB * BS
QR = 2
QN = RB // QR
MSGS = 160

PARTS = ((0, 96), (96, 112), (208, 160), (368, 144))

ORDER = (
    -4, -52, -11, -109, -100, -75, -84, -77, -68, -43, -116, -13, -107, -36, -45, -20, 3, 10,
    -28, -3, -5, 51, -60, -51, 108, -101, -110, -117, -53, 99, 74, -74, -83, -10, 83, 76, -69,
    42, 67, 12, -14, -92, -67, 115, -124, 35, 44, 106, 19, -37, -19, -35, -78, -115, -99, -85,
    128, 27, 2, 4, -2, -106, 59, -61, -29, -46, -21, 50, 100, 109, -111, 116, -125, -118, 52,
    73, -66, -73, -102, -82, 68, -93, 82, 13, 9, 91, 36, 18, -18, -27, 123, 34, 66, 77, 114,
    -79, -70, -123, -86, 1, -1, -59, -34, 60, 98, 84, 105, -98, -114, 28, -30, 65, 124, -90, 45,
    -47, 72, -80, 20, -22, -62, 101, 117, 17, -17, 129, 26, -26, -105, 110, -119, -103, -112,
    -126, -54, -38, -15, 92, 81, 0, 78, -71, -87, -65, -81, 58, 122, -58, 69, 29, 33, -33, -42,
    85, 97, 46, 21, 79, -72, -23, -91, 113, -122, 89, 16, -24, -50, 61, -63, -6, 118, 25, 102,
    -25, -9, -8, 111, -120, -104, 125, 104, -113, -97, -127, -88, 70, 53, -55, 57, 37, 86, -39,
    -31, -48, 64, -89, 32, 14, 80, 71, 41, 22, -41, -96, -57, -95, -94, 130, 23, 62, 121, -64,
    90, 49, 5, -49, -7, 119, -128, 103, 24, -32, 54, -56, 112, 8, -121, -16, 38, -40, 96, 7, 30,
    126, 88, 40, 47, 87, 56, 63, 95, 48, 6, 127, 94, 31, 55, 15, 120, 39, 93,
)


def kernel(mx_hbm, msq_hbm, mo_hbm, x_hbm, out_ref, mx, msq, mo, x_ref, panel, xc, sb, acc,
           at_v, ct_v, at_s, ct_s, send_sem, recv_sem, local_sem):
    x = lax.axis_index("row")
    c = lax.axis_index("col")
    d = lax.axis_index("depth")
    z, y = c // NY, c % NY
    e = 1 - d

    def yy(k):
        return (y + (k + NY)) % NY

    def zz(k):
        return (z + (k + NZ)) % NZ

    def xx(k):
        return (x + (k + NX)) % NX

    def dev(dx=0, dy=0, dz=0, core=None):
        return {
            "row": xx(dx) if dx else x,
            "col": (zz(dz) if dz else z) * NY + (yy(dy) if dy else y),
            "depth": d if core is None else core,
        }

    yp, ym, zp, zm = dev(dy=1), dev(dy=-1), dev(dz=1), dev(dz=-1)
    xp, xm, x2, sib = dev(dx=1), dev(dx=-1), dev(dx=2), dev(core=e)
    y2, zpp, zmm = dev(dy=2), dev(dz=2), dev(dz=-2)
    partners = (zp, zm, yp, ym, zpp, zmm, y2, xp, xm, x2, sib)

    barrier = pltpu.get_barrier_semaphore()
    for partner in partners:
        pl.semaphore_signal(
            barrier, inc=1, device_id=partner, device_id_type=pl.DeviceIdType.MESH
        )

    inputs = [
        pltpu.make_async_copy(src, dst, local_sem.at[2 + n])
        for n, (src, dst) in enumerate(
            ((mx_hbm, mx), (msq_hbm, msq), (mo_hbm, mo), (x_hbm, x_ref))
        )
    ]
    for made in inputs:
        made.start()
    panel[pl.ds(ZERO, BS)] = jnp.zeros((BS, BS), jnp.bfloat16)
    for made in inputs:
        made.wait()

    count = jnp.int32(0)
    index = [jnp.int32(0)] * SLOTS
    lane = lax.broadcasted_iota(jnp.int32, (1, 128), 1)
    me = 2 * c + d
    entry = jnp.full((1, 128), ZERO // BS, jnp.int32)
    for i in range(RB):
        keep = jnp.minimum(mx[i], 1)
        for s in range(SLOTS):
            here = jnp.maximum(1 - jnp.abs(count - s), 0)
            index[s] = index[s] + i * keep * here
        at = keep * (me * SLOTS + count) + (1 - keep) * (ZERO // BS)
        entry = jnp.where(lane == i, at, entry)
        count = count + keep
    column = jnp.full((1, 128), 2 * NC, jnp.int32)
    for s in range(SLOTS):
        there = jnp.minimum(jnp.maximum(count - s, 0), 1)
        k = there * (x * RB + index[s]) + (1 - there) * (2 * NC)
        column = jnp.where(lane == s, k, column)
    at_v[2 * c + d] = entry
    for core in range(2):
        at_v[2 * NC + core] = jnp.full((1, 128), ZERO // BS, jnp.int32)
    ct_v[x] = column
    for s in range(SLOTS):
        piece = x_ref[pl.ds(index[s] * BS, BS)]
        panel[pl.ds(pl.multiple_of(me * PACK + s * BS, BS), BS)] = piece
        xc[pl.ds(pl.multiple_of(x * PACK + s * BS, BS), BS)] = piece

    pl.semaphore_wait(barrier, len(partners))

    names = {}
    sent = {}
    together = {"s": "s", "x": "x", "c": "c", "ty": "ty", "tz": "tz", "t3": "t3", "t4": "t3"}

    def copy(name, src, dst, target):
        key = together.get(name[0], together.get(name[:2], name))
        m = names.setdefault(key, len(names))
        kind = {"s": 1, "t": 3, "c": 3}.get(name[0], 0)
        made = pltpu.make_async_remote_copy(
            src_ref=src, dst_ref=dst, send_sem=send_sem.at[kind], recv_sem=recv_sem.at[m],
            device_id=target, device_id_type=pl.DeviceIdType.MESH,
        )
        return made, kind

    def send(name, ref, target):
        made, kind = copy(name, ref, ref, target)
        made.start()
        sent[kind] = sent.get(kind, 0) + ref.shape[0]

    def recv(name, ref, target):
        copy(name, ref, ref, target)[0].wait_recv()

    def pack(core, v, k, first=0, rows=PACK):
        column = (zz(k) * NY + yy(v)) * 2 + core
        return panel.at[pl.ds(pl.multiple_of(column * PACK + first, 16), rows)]

    def share(name, ref_of):
        send("s" + name, ref_of(d), sib)

    def entries(y_):
        return at_v.at[pl.ds(pl.multiple_of((z * NY + y_) * 2, 2), 2)]

    def table(z_):
        return at_v.at[pl.ds(pl.multiple_of(z_ * (2 * NY), 2), 2 * NY)]

    def chunk(part, v, k, core=None):
        return pack(d if core is None else core, v, k, *PARTS[part])

    def step_of(part, v, k):
        far = part % 2
        if (k != 0) if part < 2 else (v == 0):
            if k < 0 or (k == 4 and not far):
                return (v, k + 1 if k < 0 else -3), zp
            return (v, k - 1), zm
        if v < 0 or (v == 2 and not far):
            return (v + 1 if v < 0 else -1, k), yp
        return (v - 1, k), ym

    def name_of(part, v, k):
        return f"{part},{v},{k}"

    def send_chunk(part, v, k):
        (pv, pk), target = step_of(part, v, k)
        send(name_of(part, v, k), chunk(part, pv, pk), target)

    def recv_chunk(part, v, k):
        recv(name_of(part, v, k), chunk(part, v, k), step_of(part, v, k)[1])
        arrived(part, v, k)

    def arrived(part, v, k):
        share(f"{part},{v},{k}", lambda core: chunk(part, v, k, core))

    for part in range(4):
        arrived(part, 0, 0)
    send("t0", at_v.at[2 * c + d], sib)
    own = xc.at[pl.ds(pl.multiple_of(x * PACK, BS), PACK)]
    for name, target in (("x+", xp), ("x-", xm), ("x2", x2)):
        send("c" + name, ct_v.at[x], target)
        send(name, own, target)
    started = False
    for n in ORDER:
        if n < 128:
            m = n if n >= 0 else -1 - n
            place = (m // 32, m // 8 % 4 - 1, m % 8 - 3)
            if n >= 0 and not started:
                started = True
                recv("t0", at_v.at[2 * c + e], sib)
                for name, target in (("ty+", yp), ("ty-", ym), ("ty2", y2)):
                    send(name, entries(y), target)
            if n >= 0:
                recv_chunk(*place)
            else:
                send_chunk(*place)
        elif n == 128:
            recv("ty", at_v.at[pl.ds(0, 3 * 2)], yp)
            for name, target in (("tz+", zp), ("tz-", zm), ("tzz+", zpp), ("tzz-", zmm)):
                send(name, table(z), target)
        elif n == 129:
            recv("tz", at_v.at[pl.ds(0, 4 * 2 * NY)], zp)
            send("t3+", table(zz(-1)), zpp)
            send("t3-", table(zz(1)), zmm)
            send("t4", table(zz(-2)), zpp)
        else:
            recv("t3", at_v.at[pl.ds(0, 3 * 2 * NY)], zpp)
    recv("c", ct_v.at[pl.ds(0, 3)], xp)
    recv("x", xc.at[pl.ds(0, 3 * PACK)], xp)
    tables = [
        pltpu.make_async_copy(at_v, at_s, local_sem.at[0]),
        pltpu.make_async_copy(ct_v, ct_s, local_sem.at[1]),
    ]
    for made in tables:
        made.start()
    recv("s", panel.at[pl.ds(0, NC * PACK)], sib)
    for made in tables:
        made.wait()

    def block(k, i):
        return panel[pl.ds(at_s[k, 0, i] * BS, BS)]

    def tile(rows, columns):
        return jnp.concatenate(
            [jnp.concatenate([block(k, i) for k in columns], axis=1) for i in rows], axis=0
        )

    def masked(flag, values):
        return jnp.where(jnp.full(values.shape, flag, jnp.int32) != 0, values, 0.0)

    def s_ref(group_, q, half=None):
        first, rows = QS[q] * BS, QL[q] * BS
        if half is not None:
            rows //= 2
            first += half * rows
        return sb.at[pl.ds(pl.multiple_of(group_ * ROWS + first, BS), rows)]

    qrows = QR * BS
    first_q = len(names)

    def chunk_copy(group_, q, target, half=None):
        rows = qrows if half is None else qrows // 2
        first = 0 if half is None else half * rows
        ref = sb.at[pl.ds(pl.multiple_of(group_ * ROWS + q * qrows + first, BS), rows)]
        return pltpu.make_async_remote_copy(
            src_ref=ref, dst_ref=ref, send_sem=send_sem.at[2],
            recv_sem=recv_sem.at[first_q + q + (0 if half is None else QN)],
            device_id=target, device_id_type=pl.DeviceIdType.MESH,
        )

    def chunk_wait(q, forwarded):
        whole = sb.at[pl.ds(0, qrows if forwarded else 2 * qrows)]
        pltpu.make_async_remote_copy(
            src_ref=whole, dst_ref=whole, send_sem=send_sem.at[2],
            recv_sem=recv_sem.at[first_q + q + (QN if forwarded else 0)],
            device_id=xp, device_id_type=pl.DeviceIdType.MESH,
        ).wait_recv()

    kept = [ct_s[j // SLOTS, 0, j % SLOTS] for j in range(NX * SLOTS)]

    def square(q, carry):
        rows = [q * QR + i for i in range(QR)]
        total = None
        for p in range(NX * SLOTS // 2):
            term = jnp.dot(
                tile(rows, kept[2 * p : 2 * p + 2]),
                xc[pl.ds(p * 2 * BS, 2 * BS)],
                preferred_element_type=jnp.float32,
            )
            total = term if total is None else total + term
        for i, row in enumerate(rows):
            part = masked(msq[row], total[i * BS : (i + 1) * BS])
            sb[pl.ds(pl.multiple_of(x * ROWS + row * BS, BS), BS)] = part.astype(jnp.bfloat16)
        chunk_copy(x, q, xp).start()
        chunk_copy(x, q, xm).start()
        return carry

    lax.fori_loop(0, QN, square, 0)
    acc[...] = jnp.zeros_like(acc)

    def cube(group_, q):
        w = sb[pl.ds(pl.multiple_of(group_ * ROWS + q * qrows, BS), qrows)]
        columns = [group_ * RB + q * QR + k for k in range(QR)]
        acc[...] += jnp.dot(
            tile(range(RB), columns), w, preferred_element_type=jnp.float32
        )

    def own_chunk(q, carry):
        cube(x, q)
        return carry

    lax.fori_loop(0, QN, own_chunk, 0)

    def near_chunk(q, carry):
        chunk_wait(q, False)
        chunk_copy(xx(-1), q, xp, 0).start()
        chunk_copy(xx(1), q, xm, 1).start()

        def side(k, carry):
            cube(xx(2 * k - 1), q)
            return carry

        return lax.fori_loop(0, 2, side, carry)

    lax.fori_loop(0, QN, near_chunk, 0)

    def far_chunk(q, carry):
        chunk_wait(q, True)
        cube(xx(2), q)
        return carry

    lax.fori_loop(0, QN, far_chunk, 0)
    sent[2] = 3 * ROWS

    for i in range(RB):
        spot = pl.ds(i * BS, BS)
        own_x = masked(mx[i], x_ref[spot].astype(jnp.float32))
        result = masked(mo[i], 1.5 * own_x - 0.5 * acc[spot])
        out_ref[spot] = result.astype(jnp.bfloat16)

    for kind, buffer in ((0, panel), (1, panel), (2, sb), (3, at_v)):
        if kind in sent:
            whole = buffer.at[pl.ds(0, sent[kind])]
            pltpu.make_async_remote_copy(
                src_ref=whole, dst_ref=whole, send_sem=send_sem.at[kind], recv_sem=recv_sem.at[0],
                device_id=xp, device_id_type=pl.DeviceIdType.MESH,
            ).wait_send()


def body(xmat, mask_x, mask_sq, mask_out):
    hbm = pl.BlockSpec(memory_space=pltpu.HBM)
    vmem = pl.BlockSpec(memory_space=pltpu.VMEM)
    return pl.pallas_call(
        kernel,
        out_shape=jax.ShapeDtypeStruct(xmat.shape, jnp.bfloat16),
        in_specs=[hbm] * 4,
        out_specs=vmem,
        scratch_shapes=[
            pltpu.SMEM((RB,), jnp.int32),
            pltpu.SMEM((RB,), jnp.int32),
            pltpu.SMEM((RB,), jnp.int32),
            pltpu.VMEM((ROWS, BS), jnp.bfloat16),
            pltpu.VMEM((ZERO + BS, BS), jnp.bfloat16),
            pltpu.VMEM((NX * PACK, BS), jnp.bfloat16),
            pltpu.VMEM((NX * ROWS, BS), jnp.bfloat16),
            pltpu.VMEM((ROWS, BS), jnp.float32),
            pltpu.VMEM((2 * NC + 2, 1, 128), jnp.int32),
            pltpu.VMEM((NX, 1, 128), jnp.int32),
            pltpu.SMEM((2 * NC + 2, 1, 128), jnp.int32),
            pltpu.SMEM((NX, 1, 128), jnp.int32),
            pltpu.SemaphoreType.DMA((4,)),
            pltpu.SemaphoreType.DMA((MSGS,)),
            pltpu.SemaphoreType.DMA((6,)),
        ],
        compiler_params=pltpu.CompilerParams(
            collective_id=0, has_side_effects=True, vmem_limit_bytes=60 * 1024 * 1024
        ),
    )(mask_x.reshape(RB), mask_sq.reshape(RB), mask_out.reshape(RB), xmat)


def solution(mesh):
    placed = P("row", ("col", "depth"))
    return jax.shard_map(
        body, mesh=mesh, in_specs=(placed,) * 4, out_specs=placed, check_vma=False
    )
```

```python
import jax
import jax.numpy as jnp
from jax import lax
from jax.experimental import pallas as pl
from jax.experimental.pallas import tpu as pltpu
from jax.sharding import PartitionSpec as P

BS = 128
RB = 16
SLOTS = 4
NX, NY, NZ = 4, 4, 8
NC = NY * NZ
PACK = SLOTS * BS
ZERO = 2 * NC * PACK
ROWS = RB * BS
QR = 2
QN = RB // QR
MSGS = 112

PARTS = ((0, 96), (96, 112), (208, 160), (368, 144))

ORDER = (
    -4, -52, -11, -109, -100, -75, -84, -77, -68, -43, -116, -13, -107, -36, -45, -20, 3, 10,
    -28, -3, -5, 51, -60, -51, 108, -101, -110, -117, -53, 99, 74, -74, -83, -10, 83, 76, -69,
    42, 67, 12, -14, -92, -67, 115, -124, 35, 44, 106, 19, -37, -19, -35, -78, -115, -99, -85,
    128, 27, 2, 4, -2, -106, 59, -61, -29, -46, -21, 50, 100, 109, -111, 116, -125, -118, 52,
    73, -66, -73, -102, -82, 68, -93, 82, 13, 9, 91, 36, 18, -18, -27, 123, 34, 66, 77, 114,
    -79, -70, -123, -86, 1, -1, -59, -34, 60, 98, 84, 105, -98, -114, 28, -30, 65, 124, -90, 45,
    -47, 72, -80, 20, -22, -62, 101, 117, 17, -17, 129, 26, -26, -105, 110, -119, -103, -112,
    -126, -54, -38, -15, 92, 81, 0, 78, -71, -87, -65, -81, 58, 122, -58, 69, 29, 33, -33, -42,
    85, 97, 46, 21, 79, -72, -23, -91, 113, -122, 89, 16, -24, -50, 61, -63, -6, 118, 25, 102,
    -25, -9, -8, 111, -120, -104, 125, 104, -113, -97, -127, -88, 70, 53, -55, 57, 37, 86, -39,
    -31, -48, 64, -89, 32, 14, 80, 71, 41, 22, -41, -96, -57, -95, -94, 130, 23, 62, 121, -64,
    90, 49, 5, -49, -7, 119, -128, 103, 24, -32, 54, -56, 112, 8, -121, -16, 38, -40, 96, 7, 30,
    126, 88, 40, 47, 87, 56, 63, 95, 48, 6, 127, 94, 31, 55, 15, 120, 39, 93,
)


def kernel(mx_hbm, msq_hbm, mo_hbm, x_hbm, out_ref, mx, msq, mo, x_ref, panel, xc, sb, acc,
           at_v, ct_v, at_s, ct_s, send_sem, recv_sem, local_sem):
    x = lax.axis_index("row")
    c = lax.axis_index("col")
    d = lax.axis_index("depth")
    z, y = c // NY, c % NY
    e = 1 - d

    def yy(k):
        return (y + (k + NY)) % NY

    def zz(k):
        return (z + (k + NZ)) % NZ

    def xx(k):
        return (x + (k + NX)) % NX

    def dev(dx=0, dy=0, dz=0, core=None):
        return {
            "row": xx(dx) if dx else x,
            "col": (zz(dz) if dz else z) * NY + (yy(dy) if dy else y),
            "depth": d if core is None else core,
        }

    yp, ym, zp, zm = dev(dy=1), dev(dy=-1), dev(dz=1), dev(dz=-1)
    xp, xm, x2, sib = dev(dx=1), dev(dx=-1), dev(dx=2), dev(core=e)
    y2, zpp, zmm = dev(dy=2), dev(dz=2), dev(dz=-2)
    partners = (zp, zm, yp, ym, zpp, zmm, y2, xp, xm, x2, sib)

    barrier = pltpu.get_barrier_semaphore()
    for partner in partners:
        pl.semaphore_signal(
            barrier, inc=1, device_id=partner, device_id_type=pl.DeviceIdType.MESH
        )

    inputs = [
        pltpu.make_async_copy(src, dst, local_sem.at[2 + n])
        for n, (src, dst) in enumerate(
            ((mx_hbm, mx), (msq_hbm, msq), (mo_hbm, mo), (x_hbm, x_ref))
        )
    ]
    for made in inputs:
        made.start()
    panel[pl.ds(ZERO, BS)] = jnp.zeros((BS, BS), jnp.bfloat16)
    for made in inputs:
        made.wait()

    count = jnp.int32(0)
    index = [jnp.int32(0)] * SLOTS
    lane = lax.broadcasted_iota(jnp.int32, (1, 128), 1)
    me = 2 * c + d
    entry = jnp.full((1, 128), ZERO // BS, jnp.int32)
    for i in range(RB):
        keep = jnp.minimum(mx[i], 1)
        for s in range(SLOTS):
            here = jnp.maximum(1 - jnp.abs(count - s), 0)
            index[s] = index[s] + i * keep * here
        at = keep * (me * SLOTS + count) + (1 - keep) * (ZERO // BS)
        entry = jnp.where(lane == i, at, entry)
        count = count + keep
    column = jnp.full((1, 128), 2 * NC, jnp.int32)
    for s in range(SLOTS):
        there = jnp.minimum(jnp.maximum(count - s, 0), 1)
        k = there * (x * RB + index[s]) + (1 - there) * (2 * NC)
        column = jnp.where(lane == s, k, column)
    at_v[2 * c + d] = entry
    for core in range(2):
        at_v[2 * NC + core] = jnp.full((1, 128), ZERO // BS, jnp.int32)
    ct_v[x] = column
    for s in range(SLOTS):
        piece = x_ref[pl.ds(index[s] * BS, BS)]
        panel[pl.ds(pl.multiple_of(me * PACK + s * BS, BS), BS)] = piece
        xc[pl.ds(pl.multiple_of(x * PACK + s * BS, BS), BS)] = piece

    pl.semaphore_wait(barrier, len(partners))

    names = {}
    sent = {}
    together = {"s": "s", "x": "x", "c": "c", "ty": "ty", "tz": "tz", "t3": "t3", "t4": "t3"}

    def copy(name, src, dst, target):
        key = together.get(name[0], together.get(name[:2], together.get(name, name)))
        m = names.setdefault(key, len(names))
        kind = {"s": 1, "t": 3, "c": 3}.get(name[0], 0)
        made = pltpu.make_async_remote_copy(
            src_ref=src, dst_ref=dst, send_sem=send_sem.at[kind], recv_sem=recv_sem.at[m],
            device_id=target, device_id_type=pl.DeviceIdType.MESH,
        )
        return made, kind

    def send(name, ref, target):
        made, kind = copy(name, ref, ref, target)
        made.start()
        sent[kind] = sent.get(kind, 0) + ref.shape[0]

    def recv(name, ref, target):
        copy(name, ref, ref, target)[0].wait_recv()

    def pack(core, v, k, first=0, rows=PACK):
        column = (zz(k) * NY + yy(v)) * 2 + core
        return panel.at[pl.ds(pl.multiple_of(column * PACK + first, 16), rows)]

    def share(name, ref_of):
        send("s" + name, ref_of(d), sib)

    def entries(y_):
        return at_v.at[pl.ds(pl.multiple_of((z * NY + y_) * 2, 2), 2)]

    def table(z_):
        return at_v.at[pl.ds(pl.multiple_of(z_ * (2 * NY), 2), 2 * NY)]

    def chunk(part, v, k, core=None):
        return pack(d if core is None else core, v, k, *PARTS[part])

    def step_of(part, v, k):
        far = part % 2
        if (k != 0) if part < 2 else (v == 0):
            if k < 0 or (k == 4 and not far):
                return (v, k + 1 if k < 0 else -3), zp
            return (v, k - 1), zm
        if v < 0 or (v == 2 and not far):
            return (v + 1 if v < 0 else -1, k), yp
        return (v - 1, k), ym

    def name_of(part, v, k):
        return f"{part},{v},{k}"

    def send_chunk(part, v, k):
        (pv, pk), target = step_of(part, v, k)
        send(name_of(part, v, k), chunk(part, pv, pk), target)

    def arrived(part, v, k):
        share(f"{part},{v},{k}", lambda core: chunk(part, v, k, core))

    def place(n):
        return n // 32, n // 8 % 4 - 1, n % 8 - 3

    runs = []
    for n, before in zip(ORDER, (-1,) + ORDER):
        if 0 <= n < 128:
            if not 0 <= before < 128 or len(runs[-1]) == 2:
                runs.append([])
            runs[-1].append(place(n))
    for number, run in enumerate(runs):
        for one in run:
            together[name_of(*one)] = f"run{number}"

    send("t0", at_v.at[2 * c + d], sib)
    begun = 0
    for n in ORDER:
        if n < 0:
            send_chunk(*place(-1 - n))
        elif n < 128:
            if begun == len(runs) or place(n) != runs[begun][0]:
                continue
            if begun == 0:
                for part in range(4):
                    arrived(part, 0, 0)
                recv("t0", at_v.at[2 * c + e], sib)
                for name, target in (("ty+", yp), ("ty-", ym), ("ty2", y2)):
                    send(name, entries(y), target)
                own = xc.at[pl.ds(pl.multiple_of(x * PACK, BS), PACK)]
                for name, target in (("x+", xp), ("x-", xm), ("x2", x2)):
                    send("c" + name, ct_v.at[x], target)
                    send(name, own, target)
            run = runs[begun]
            begun += 1
            total = sum(PARTS[part][1] for part, _, _ in run)
            recv(name_of(*run[0]), panel.at[pl.ds(0, total)], yp)
            for one in run:
                arrived(*one)
        elif n == 128:
            recv("ty", at_v.at[pl.ds(0, 3 * 2)], yp)
            for name, target in (("tz+", zp), ("tz-", zm), ("tzz+", zpp), ("tzz-", zmm)):
                send(name, table(z), target)
        elif n == 129:
            recv("tz", at_v.at[pl.ds(0, 4 * 2 * NY)], zp)
            send("t3+", table(zz(-1)), zpp)
            send("t3-", table(zz(1)), zmm)
            send("t4", table(zz(-2)), zpp)
        else:
            recv("t3", at_v.at[pl.ds(0, 3 * 2 * NY)], zpp)
    recv("c", ct_v.at[pl.ds(0, 3)], xp)
    recv("x", xc.at[pl.ds(0, 3 * PACK)], xp)
    tables = [
        pltpu.make_async_copy(at_v, at_s, local_sem.at[0]),
        pltpu.make_async_copy(ct_v, ct_s, local_sem.at[1]),
    ]
    for made in tables:
        made.start()
    recv("s", panel.at[pl.ds(0, NC * PACK)], sib)
    for made in tables:
        made.wait()

    def block(k, i):
        return panel[pl.ds(at_s[k, 0, i] * BS, BS)]

    def tile(rows, columns):
        return jnp.concatenate(
            [jnp.concatenate([block(k, i) for k in columns], axis=1) for i in rows], axis=0
        )

    def masked(flag, values):
        return jnp.where(jnp.full(values.shape, flag, jnp.int32) != 0, values, 0.0)

    def s_ref(group_, q, half=None):
        first, rows = QS[q] * BS, QL[q] * BS
        if half is not None:
            rows //= 2
            first += half * rows
        return sb.at[pl.ds(pl.multiple_of(group_ * ROWS + first, BS), rows)]

    qrows = QR * BS
    first_q = len(names)

    def chunk_copy(group_, q, target, half=None):
        rows = qrows if half is None else qrows // 2
        first = 0 if half is None else half * rows
        ref = sb.at[pl.ds(pl.multiple_of(group_ * ROWS + q * qrows + first, BS), rows)]
        return pltpu.make_async_remote_copy(
            src_ref=ref, dst_ref=ref, send_sem=send_sem.at[2],
            recv_sem=recv_sem.at[first_q + q + (0 if half is None else QN)],
            device_id=target, device_id_type=pl.DeviceIdType.MESH,
        )

    def chunk_wait(q, forwarded):
        whole = sb.at[pl.ds(0, qrows if forwarded else 2 * qrows)]
        pltpu.make_async_remote_copy(
            src_ref=whole, dst_ref=whole, send_sem=send_sem.at[2],
            recv_sem=recv_sem.at[first_q + q + (QN if forwarded else 0)],
            device_id=xp, device_id_type=pl.DeviceIdType.MESH,
        ).wait_recv()

    kept = [ct_s[j // SLOTS, 0, j % SLOTS] for j in range(NX * SLOTS)]

    def square(q, carry):
        rows = [q * QR + i for i in range(QR)]
        total = None
        for p in range(NX * SLOTS // 2):
            term = jnp.dot(
                tile(rows, kept[2 * p : 2 * p + 2]),
                xc[pl.ds(p * 2 * BS, 2 * BS)],
                preferred_element_type=jnp.float32,
            )
            total = term if total is None else total + term
        for i, row in enumerate(rows):
            part = masked(msq[row], total[i * BS : (i + 1) * BS])
            sb[pl.ds(pl.multiple_of(x * ROWS + row * BS, BS), BS)] = part.astype(jnp.bfloat16)
        chunk_copy(x, q, xp).start()
        chunk_copy(x, q, xm).start()
        return carry

    lax.fori_loop(0, QN, square, 0)
    acc[...] = jnp.zeros_like(acc)

    def cube(group_, q):
        w = sb[pl.ds(pl.multiple_of(group_ * ROWS + q * qrows, BS), qrows)]
        columns = [group_ * RB + q * QR + k for k in range(QR)]
        acc[...] += jnp.dot(
            tile(range(RB), columns), w, preferred_element_type=jnp.float32
        )

    def own_chunk(q, carry):
        cube(x, q)
        return carry

    lax.fori_loop(0, QN, own_chunk, 0)

    def near_chunk(q, carry):
        chunk_wait(q, False)
        chunk_copy(xx(-1), q, xp, 0).start()
        chunk_copy(xx(1), q, xm, 1).start()

        def side(k, carry):
            cube(xx(2 * k - 1), q)
            return carry

        return lax.fori_loop(0, 2, side, carry)

    lax.fori_loop(0, QN, near_chunk, 0)

    def far_chunk(q, carry):
        chunk_wait(q, True)
        cube(xx(2), q)
        return carry

    lax.fori_loop(0, QN, far_chunk, 0)
    sent[2] = 3 * ROWS

    for i in range(RB):
        spot = pl.ds(i * BS, BS)
        own_x = masked(mx[i], x_ref[spot].astype(jnp.float32))
        result = masked(mo[i], 1.5 * own_x - 0.5 * acc[spot])
        out_ref[spot] = result.astype(jnp.bfloat16)

    for kind, buffer in ((0, panel), (1, panel), (2, sb), (3, at_v)):
        if kind in sent:
            whole = buffer.at[pl.ds(0, sent[kind])]
            pltpu.make_async_remote_copy(
                src_ref=whole, dst_ref=whole, send_sem=send_sem.at[kind], recv_sem=recv_sem.at[0],
                device_id=xp, device_id_type=pl.DeviceIdType.MESH,
            ).wait_send()


def body(xmat, mask_x, mask_sq, mask_out):
    hbm = pl.BlockSpec(memory_space=pltpu.HBM)
    vmem = pl.BlockSpec(memory_space=pltpu.VMEM)
    return pl.pallas_call(
        kernel,
        out_shape=jax.ShapeDtypeStruct(xmat.shape, jnp.bfloat16),
        in_specs=[hbm] * 4,
        out_specs=vmem,
        scratch_shapes=[
            pltpu.SMEM((RB,), jnp.int32),
            pltpu.SMEM((RB,), jnp.int32),
            pltpu.SMEM((RB,), jnp.int32),
            pltpu.VMEM((ROWS, BS), jnp.bfloat16),
            pltpu.VMEM((ZERO + BS, BS), jnp.bfloat16),
            pltpu.VMEM((NX * PACK, BS), jnp.bfloat16),
            pltpu.VMEM((NX * ROWS, BS), jnp.bfloat16),
            pltpu.VMEM((ROWS, BS), jnp.float32),
            pltpu.VMEM((2 * NC + 2, 1, 128), jnp.int32),
            pltpu.VMEM((NX, 1, 128), jnp.int32),
            pltpu.SMEM((2 * NC + 2, 1, 128), jnp.int32),
            pltpu.SMEM((NX, 1, 128), jnp.int32),
            pltpu.SemaphoreType.DMA((4,)),
            pltpu.SemaphoreType.DMA((MSGS,)),
            pltpu.SemaphoreType.DMA((6,)),
        ],
        compiler_params=pltpu.CompilerParams(
            collective_id=0, has_side_effects=True, vmem_limit_bytes=53 * 1024 * 1024
        ),
    )(mask_x.reshape(RB), mask_sq.reshape(RB), mask_out.reshape(RB), xmat)


def solution(mesh):
    placed = P("row", ("col", "depth"))
    return jax.shard_map(
        body, mesh=mesh, in_specs=(placed,) * 4, out_specs=placed, check_vma=False
    )
```

```python
import jax
import jax.numpy as jnp
from jax import lax
from jax.experimental import pallas as pl
from jax.experimental.pallas import tpu as pltpu
from jax.sharding import PartitionSpec as P

BS = 128
RB = 16
SLOTS = 4
NX, NY, NZ = 4, 4, 8
NC = NY * NZ
PACK = SLOTS * BS
ZERO = 2 * NC * PACK
ROWS = RB * BS
QR = 2
QN = RB // QR
MSGS = 102

PARTS = ((0, 112), (112, 96), (208, 144), (352, 160))

ORDER = (
    -4, -52, -11, -77, -84, -100, -75, -109, -116, -43, -36, -13, -107, -68, -20, -45, 51, -60,
    -51, -53, 3, 10, -28, -3, 76, -85, -78, -69, 83, 74, -74, 99, 108, -117, -110, -101, 42, 35,
    -35, 115, -124, 12, -14, -37, 67, 19, 106, 44, -92, -19, -115, -106, -67, -99, -83, 128, 59,
    50, 52, -61, -54, 27, -27, -29, 2, -2, 84, 77, -70, -79, 68, 73, -82, -73, -66, -93, 116,
    109, -125, -111, -86, 100, 34, 13, 123, 18, -18, -50, 91, 36, 60, -62, 114, 105, 66, -105,
    -91, -114, -102, -123, 53, -55, 26, -26, 82, 98, 28, -30, -46, -21, -38, 1, -1, 81, 69, 78,
    -87, 72, -65, -80, 124, 65, -90, 17, -17, -59, -10, 110, -119, -112, -103, -118, -5, -15,
    129, 49, 92, 85, 61, 54, 104, 90, -97, -113, -71, -81, 113, 29, 25, -25, -34, -42, 45, 101,
    -47, 122, 0, 20, -22, 64, 86, 37, 79, -72, -88, -39, -63, 89, 16, 118, -24, 111, -104, -120,
    -89, -98, 58, -58, 102, 117, 4, -6, -126, -31, 9, -9, 14, 96, 112, 24, -32, -121, -127,
    -122, 46, -48, 33, -33, 70, -95, 80, 21, -23, 41, -41, -49, 130, 38, 71, -40, -96, -94, 87,
    23, 62, -64, 57, -57, 103, 119, -128, 5, -7, -56, 8, -16, -8, 88, 30, 125, 31, 47, 32, 97,
    120, 22, 40, 94, 39, 48, 126, 63, 95, 56, 121, 6, 15, 93, 55, 7, 127,
)


def kernel(mx_hbm, msq_hbm, mo_hbm, x_hbm, out_ref, mx, msq, mo, x_ref, panel, xc, sb, acc,
           at_v, ct_v, at_s, ct_s, send_sem, recv_sem, local_sem):
    x = lax.axis_index("row")
    c = lax.axis_index("col")
    d = lax.axis_index("depth")
    z, y = c // NY, c % NY
    e = 1 - d

    def yy(k):
        return (y + (k + NY)) % NY

    def zz(k):
        return (z + (k + NZ)) % NZ

    def xx(k):
        return (x + (k + NX)) % NX

    def dev(dx=0, dy=0, dz=0, core=None):
        return {
            "row": xx(dx) if dx else x,
            "col": (zz(dz) if dz else z) * NY + (yy(dy) if dy else y),
            "depth": d if core is None else core,
        }

    yp, ym, zp, zm = dev(dy=1), dev(dy=-1), dev(dz=1), dev(dz=-1)
    xp, xm, x2, sib = dev(dx=1), dev(dx=-1), dev(dx=2), dev(core=e)
    y2, zpp, zmm = dev(dy=2), dev(dz=2), dev(dz=-2)
    partners = (zp, zm, yp, ym, zpp, zmm, y2, xp, xm, x2, sib)

    barrier = pltpu.get_barrier_semaphore()
    for partner in partners:
        pl.semaphore_signal(
            barrier, inc=1, device_id=partner, device_id_type=pl.DeviceIdType.MESH
        )

    inputs = [
        pltpu.make_async_copy(src, dst, local_sem.at[2 + n])
        for n, (src, dst) in enumerate(
            ((mx_hbm, mx), (msq_hbm, msq), (mo_hbm, mo), (x_hbm, x_ref))
        )
    ]
    for made in inputs:
        made.start()
    panel[pl.ds(ZERO, BS)] = jnp.zeros((BS, BS), jnp.bfloat16)
    for made in inputs:
        made.wait()

    count = jnp.int32(0)
    index = [jnp.int32(0)] * SLOTS
    lane = lax.broadcasted_iota(jnp.int32, (1, 128), 1)
    me = 2 * c + d
    entry = jnp.full((1, 128), ZERO // BS, jnp.int32)
    for i in range(RB):
        keep = jnp.minimum(mx[i], 1)
        for s in range(SLOTS):
            here = jnp.maximum(1 - jnp.abs(count - s), 0)
            index[s] = index[s] + i * keep * here
        at = keep * (me * SLOTS + count) + (1 - keep) * (ZERO // BS)
        entry = jnp.where(lane == i, at, entry)
        count = count + keep
    column = jnp.full((1, 128), 2 * NC, jnp.int32)
    for s in range(SLOTS):
        there = jnp.minimum(jnp.maximum(count - s, 0), 1)
        k = there * (x * RB + index[s]) + (1 - there) * (2 * NC)
        column = jnp.where(lane == s, k, column)
    at_v[2 * c + d] = entry
    for core in range(2):
        at_v[2 * NC + core] = jnp.full((1, 128), ZERO // BS, jnp.int32)
    ct_v[x] = column
    for s in range(SLOTS):
        piece = x_ref[pl.ds(index[s] * BS, BS)]
        panel[pl.ds(pl.multiple_of(me * PACK + s * BS, BS), BS)] = piece
        xc[pl.ds(pl.multiple_of(x * PACK + s * BS, BS), BS)] = piece

    pl.semaphore_wait(barrier, len(partners))

    names = {}
    sent = {}
    together = {"s": "s", "x": "x", "c": "c", "ty": "ty", "tz": "tz", "t3": "t3", "t4": "t3"}

    def copy(name, src, dst, target):
        key = together.get(name[0], together.get(name[:2], together.get(name, name)))
        m = names.setdefault(key, len(names))
        kind = {"s": 1, "t": 3, "c": 3}.get(name[0], 0)
        made = pltpu.make_async_remote_copy(
            src_ref=src, dst_ref=dst, send_sem=send_sem.at[kind], recv_sem=recv_sem.at[m],
            device_id=target, device_id_type=pl.DeviceIdType.MESH,
        )
        return made, kind

    def send(name, ref, target):
        made, kind = copy(name, ref, ref, target)
        made.start()
        sent[kind] = sent.get(kind, 0) + ref.shape[0]

    def recv(name, ref, target):
        copy(name, ref, ref, target)[0].wait_recv()

    def pack(core, v, k, first=0, rows=PACK):
        column = (zz(k) * NY + yy(v)) * 2 + core
        return panel.at[pl.ds(pl.multiple_of(column * PACK + first, 16), rows)]

    def share(name, ref_of):
        send("s" + name, ref_of(d), sib)

    def entries(y_):
        return at_v.at[pl.ds(pl.multiple_of((z * NY + y_) * 2, 2), 2)]

    def table(z_):
        return at_v.at[pl.ds(pl.multiple_of(z_ * (2 * NY), 2), 2 * NY)]

    def chunk(part, v, k, core=None):
        return pack(d if core is None else core, v, k, *PARTS[part])

    def step_of(part, v, k):
        far = part % 2
        if (k != 0) if part < 2 else (v == 0):
            if k < 0 or (k == 4 and not far):
                return (v, k + 1 if k < 0 else -3), zp
            return (v, k - 1), zm
        if v < 0 or (v == 2 and not far):
            return (v + 1 if v < 0 else -1, k), yp
        return (v - 1, k), ym

    def name_of(part, v, k):
        return f"{part},{v},{k}"

    def send_chunk(part, v, k):
        (pv, pk), target = step_of(part, v, k)
        send(name_of(part, v, k), chunk(part, pv, pk), target)

    def arrived(part, v, k):
        share(f"{part},{v},{k}", lambda core: chunk(part, v, k, core))

    def place(n):
        return n // 32, n // 8 % 4 - 1, n % 8 - 3

    runs = []
    for n, before in zip(ORDER, (-1,) + ORDER):
        if 0 <= n < 128:
            if not 0 <= before < 128 or len(runs[-1]) == 2:
                runs.append([])
            runs[-1].append(place(n))
    for number, run in enumerate(runs):
        for one in run:
            together[name_of(*one)] = f"run{number}"

    send("t0", at_v.at[2 * c + d], sib)
    begun = 0
    for n in ORDER:
        if n < 0:
            send_chunk(*place(-1 - n))
        elif n < 128:
            if begun == len(runs) or place(n) != runs[begun][0]:
                continue
            if begun == 0:
                for part in range(4):
                    arrived(part, 0, 0)
                recv("t0", at_v.at[2 * c + e], sib)
                for name, target in (("ty+", yp), ("ty-", ym), ("ty2", y2)):
                    send(name, entries(y), target)
                own = xc.at[pl.ds(pl.multiple_of(x * PACK, BS), PACK)]
                for name, target in (("x+", xp), ("x-", xm), ("x2", x2)):
                    send("c" + name, ct_v.at[x], target)
                    send(name, own, target)
            run = runs[begun]
            begun += 1
            total = sum(PARTS[part][1] for part, _, _ in run)
            recv(name_of(*run[0]), panel.at[pl.ds(0, total)], yp)
            for one in run:
                arrived(*one)
        elif n == 128:
            recv("ty", at_v.at[pl.ds(0, 3 * 2)], yp)
            for name, target in (("tz+", zp), ("tz-", zm), ("tzz+", zpp), ("tzz-", zmm)):
                send(name, table(z), target)
        elif n == 129:
            recv("tz", at_v.at[pl.ds(0, 4 * 2 * NY)], zp)
            send("t3+", table(zz(-1)), zpp)
            send("t3-", table(zz(1)), zmm)
            send("t4", table(zz(-2)), zpp)
        else:
            recv("t3", at_v.at[pl.ds(0, 3 * 2 * NY)], zpp)
    recv("c", ct_v.at[pl.ds(0, 3)], xp)
    recv("x", xc.at[pl.ds(0, 3 * PACK)], xp)
    tables = [
        pltpu.make_async_copy(at_v, at_s, local_sem.at[0]),
        pltpu.make_async_copy(ct_v, ct_s, local_sem.at[1]),
    ]
    for made in tables:
        made.start()
    recv("s", panel.at[pl.ds(0, NC * PACK)], sib)
    for made in tables:
        made.wait()

    def block(k, i):
        return panel[pl.ds(at_s[k, 0, i] * BS, BS)]

    def tile(rows, columns):
        return jnp.concatenate(
            [jnp.concatenate([block(k, i) for k in columns], axis=1) for i in rows], axis=0
        )

    def masked(flag, values):
        return jnp.where(jnp.full(values.shape, flag, jnp.int32) != 0, values, 0.0)

    def s_ref(group_, q, half=None):
        first, rows = QS[q] * BS, QL[q] * BS
        if half is not None:
            rows //= 2
            first += half * rows
        return sb.at[pl.ds(pl.multiple_of(group_ * ROWS + first, BS), rows)]

    qrows = QR * BS
    first_q = len(names)

    def chunk_copy(group_, q, target, half=None):
        rows = qrows if half is None else qrows // 2
        first = 0 if half is None else half * rows
        ref = sb.at[pl.ds(pl.multiple_of(group_ * ROWS + q * qrows + first, BS), rows)]
        return pltpu.make_async_remote_copy(
            src_ref=ref, dst_ref=ref, send_sem=send_sem.at[2],
            recv_sem=recv_sem.at[first_q + q + (0 if half is None else QN)],
            device_id=target, device_id_type=pl.DeviceIdType.MESH,
        )

    def chunk_wait(q, forwarded):
        whole = sb.at[pl.ds(0, qrows if forwarded else 2 * qrows)]
        pltpu.make_async_remote_copy(
            src_ref=whole, dst_ref=whole, send_sem=send_sem.at[2],
            recv_sem=recv_sem.at[first_q + q + (QN if forwarded else 0)],
            device_id=xp, device_id_type=pl.DeviceIdType.MESH,
        ).wait_recv()

    kept = [ct_s[j // SLOTS, 0, j % SLOTS] for j in range(NX * SLOTS)]

    def square(q, carry):
        rows = [q * QR + i for i in range(QR)]
        total = None
        for p in range(NX * SLOTS // 2):
            term = jnp.dot(
                tile(rows, kept[2 * p : 2 * p + 2]),
                xc[pl.ds(p * 2 * BS, 2 * BS)],
                preferred_element_type=jnp.float32,
            )
            total = term if total is None else total + term
        for i, row in enumerate(rows):
            part = masked(msq[row], total[i * BS : (i + 1) * BS])
            sb[pl.ds(pl.multiple_of(x * ROWS + row * BS, BS), BS)] = part.astype(jnp.bfloat16)
        chunk_copy(x, q, xp).start()
        chunk_copy(x, q, xm).start()
        return carry

    lax.fori_loop(0, QN, square, 0)
    acc[...] = jnp.zeros_like(acc)

    def cube(group_, q):
        w = sb[pl.ds(pl.multiple_of(group_ * ROWS + q * qrows, BS), qrows)]
        columns = [group_ * RB + q * QR + k for k in range(QR)]
        acc[...] += jnp.dot(
            tile(range(RB), columns), w, preferred_element_type=jnp.float32
        )

    def own_chunk(q, carry):
        cube(x, q)
        return carry

    lax.fori_loop(0, QN, own_chunk, 0)

    def near_chunk(q, carry):
        chunk_wait(q, False)
        chunk_copy(xx(-1), q, xp, 0).start()
        chunk_copy(xx(1), q, xm, 1).start()

        def side(k, carry):
            cube(xx(2 * k - 1), q)
            return carry

        return lax.fori_loop(0, 2, side, carry)

    lax.fori_loop(0, QN, near_chunk, 0)

    def far_chunk(q, carry):
        chunk_wait(q, True)
        cube(xx(2), q)
        return carry

    lax.fori_loop(0, QN, far_chunk, 0)
    sent[2] = 3 * ROWS

    for i in range(RB):
        spot = pl.ds(i * BS, BS)
        own_x = masked(mx[i], x_ref[spot].astype(jnp.float32))
        result = masked(mo[i], 1.5 * own_x - 0.5 * acc[spot])
        out_ref[spot] = result.astype(jnp.bfloat16)

    for kind, buffer in ((0, panel), (1, panel), (2, sb), (3, at_v)):
        if kind in sent:
            whole = buffer.at[pl.ds(0, sent[kind])]
            pltpu.make_async_remote_copy(
                src_ref=whole, dst_ref=whole, send_sem=send_sem.at[kind], recv_sem=recv_sem.at[0],
                device_id=xp, device_id_type=pl.DeviceIdType.MESH,
            ).wait_send()


def body(xmat, mask_x, mask_sq, mask_out):
    hbm = pl.BlockSpec(memory_space=pltpu.HBM)
    vmem = pl.BlockSpec(memory_space=pltpu.VMEM)
    return pl.pallas_call(
        kernel,
        out_shape=jax.ShapeDtypeStruct(xmat.shape, jnp.bfloat16),
        in_specs=[hbm] * 4,
        out_specs=vmem,
        scratch_shapes=[
            pltpu.SMEM((RB,), jnp.int32),
            pltpu.SMEM((RB,), jnp.int32),
            pltpu.SMEM((RB,), jnp.int32),
            pltpu.VMEM((ROWS, BS), jnp.bfloat16),
            pltpu.VMEM((ZERO + BS, BS), jnp.bfloat16),
            pltpu.VMEM((NX * PACK, BS), jnp.bfloat16),
            pltpu.VMEM((NX * ROWS, BS), jnp.bfloat16),
            pltpu.VMEM((ROWS, BS), jnp.float32),
            pltpu.VMEM((2 * NC + 2, 1, 128), jnp.int32),
            pltpu.VMEM((NX, 1, 128), jnp.int32),
            pltpu.SMEM((2 * NC + 2, 1, 128), jnp.int32),
            pltpu.SMEM((NX, 1, 128), jnp.int32),
            pltpu.SemaphoreType.DMA((4,)),
            pltpu.SemaphoreType.DMA((MSGS,)),
            pltpu.SemaphoreType.DMA((6,)),
        ],
        compiler_params=pltpu.CompilerParams(
            collective_id=0, has_side_effects=True, vmem_limit_bytes=53 * 1024 * 1024
        ),
    )(mask_x.reshape(RB), mask_sq.reshape(RB), mask_out.reshape(RB), xmat)


def solution(mesh):
    placed = P("row", ("col", "depth"))
    return jax.shard_map(
        body, mesh=mesh, in_specs=(placed,) * 4, out_specs=placed, check_vma=False
    )
```

```python
import jax
import jax.numpy as jnp
from jax import lax
from jax.experimental import pallas as pl
from jax.experimental.pallas import tpu as pltpu
from jax.sharding import PartitionSpec as P

BS = 128
RB = 16
SLOTS = 4
NX, NY, NZ = 4, 4, 8
NC = NY * NZ
PACK = SLOTS * BS
ZERO = 2 * NC * PACK
ROWS = RB * BS
QR = 2
QN = RB // QR
MSGS = 102

PARTS = ((0, 112), (112, 96), (208, 144), (352, 160))

ORDER = (
    -4, -52, -11, -77, -84, -100, -75, -109, -116, -43, -36, -13, -107, -68, -20, -45, 51, -60,
    -51, -53, 3, 10, -28, -3, 76, -85, -78, -69, 83, 74, -74, 99, 108, -117, -110, -101, 42, 35,
    -35, 115, -124, 12, -14, -37, 67, 19, 106, 44, -92, -19, -115, -106, -67, -99, -83, 128, 59,
    50, 52, -61, -54, 27, -27, -29, 2, -2, 84, 77, -70, -79, 68, 73, -82, -73, -66, -93, 116,
    109, -125, -111, -86, 100, 34, 13, 123, 18, -18, -50, 91, 36, 60, -62, 114, 105, 66, -105,
    -91, -114, -102, -123, 53, -55, 26, -26, 82, 98, 28, -30, -46, -21, -38, 1, -1, 81, 69, 78,
    -87, 72, -65, -80, 124, 65, -90, 17, -17, -59, -10, 110, -119, -112, -103, -118, -5, -15,
    129, 49, 92, 85, 61, 54, 104, 90, -97, -113, -71, -81, 113, 29, 25, -25, -34, -42, 45, 101,
    -47, 122, 0, 20, -22, 64, 86, 37, 79, -72, -88, -39, -63, 89, 16, 118, -24, 111, -104, -120,
    -89, -98, 58, -58, 102, 117, 4, -6, -126, -31, 9, -9, 14, 96, 112, 24, -32, -121, -127,
    -122, 46, -48, 33, -33, 70, -95, 80, 21, -23, 41, -41, -49, 130, 38, 71, -40, -96, -94, 87,
    23, 62, -64, 57, -57, 103, 119, -128, 5, -7, -56, 8, -16, -8, 88, 30, 125, 31, 47, 32, 97,
    120, 22, 40, 94, 39, 48, 126, 63, 95, 56, 121, 6, 15, 93, 55, 7, 127,
)


def kernel(mx_hbm, msq_hbm, mo_hbm, x_hbm, out_ref, mx, msq, mo, x_ref, panel, xc, sb, acc,
           at_v, ct_v, at_s, ct_s, send_sem, recv_sem, local_sem):
    x = lax.axis_index("row")
    c = lax.axis_index("col")
    d = lax.axis_index("depth")
    z, y = c // NY, c % NY
    e = 1 - d

    def yy(k):
        return (y + (k + NY)) % NY

    def zz(k):
        return (z + (k + NZ)) % NZ

    def xx(k):
        return (x + (k + NX)) % NX

    def dev(dx=0, dy=0, dz=0, core=None):
        return {
            "row": xx(dx) if dx else x,
            "col": (zz(dz) if dz else z) * NY + (yy(dy) if dy else y),
            "depth": d if core is None else core,
        }

    yp, ym, zp, zm = dev(dy=1), dev(dy=-1), dev(dz=1), dev(dz=-1)
    xp, xm, x2, sib = dev(dx=1), dev(dx=-1), dev(dx=2), dev(core=e)
    y2, zpp, zmm = dev(dy=2), dev(dz=2), dev(dz=-2)
    partners = (zp, zm, yp, ym, zpp, zmm, y2, xp, xm, x2, sib)

    barrier = pltpu.get_barrier_semaphore()
    for partner in partners:
        pl.semaphore_signal(
            barrier, inc=1, device_id=partner, device_id_type=pl.DeviceIdType.MESH
        )

    inputs = [
        pltpu.make_async_copy(src, dst, local_sem.at[2 + n])
        for n, (src, dst) in enumerate(
            ((mx_hbm, mx), (msq_hbm, msq), (mo_hbm, mo), (x_hbm, x_ref))
        )
    ]
    for made in inputs:
        made.start()
    panel[pl.ds(ZERO, BS)] = jnp.zeros((BS, BS), jnp.bfloat16)
    for made in inputs:
        made.wait()

    count = jnp.int32(0)
    index = [jnp.int32(0)] * SLOTS
    lane = lax.broadcasted_iota(jnp.int32, (1, 128), 1)
    me = 2 * c + d
    entry = jnp.full((1, 128), ZERO // BS, jnp.int32)
    for i in range(RB):
        keep = jnp.minimum(mx[i], 1)
        for s in range(SLOTS):
            here = jnp.maximum(1 - jnp.abs(count - s), 0)
            index[s] = index[s] + i * keep * here
        at = keep * (me * SLOTS + count) + (1 - keep) * (ZERO // BS)
        entry = jnp.where(lane == i, at, entry)
        count = count + keep
    column = jnp.full((1, 128), 2 * NC, jnp.int32)
    for s in range(SLOTS):
        there = jnp.minimum(jnp.maximum(count - s, 0), 1)
        k = there * (x * RB + index[s]) + (1 - there) * (2 * NC)
        column = jnp.where(lane == s, k, column)
    at_v[2 * c + d] = entry
    for core in range(2):
        at_v[2 * NC + core] = jnp.full((1, 128), ZERO // BS, jnp.int32)
    ct_v[x] = column
    for s in range(SLOTS):
        piece = x_ref[pl.ds(index[s] * BS, BS)]
        panel[pl.ds(pl.multiple_of(me * PACK + s * BS, BS), BS)] = piece
        xc[pl.ds(pl.multiple_of(x * PACK + s * BS, BS), BS)] = piece

    pl.semaphore_wait(barrier, len(partners))

    names = {}
    sent = {}
    together = {"s": "s", "x": "x", "c": "c", "ty": "ty", "tz": "tz", "t3": "t3", "t4": "t3"}

    def copy(name, src, dst, target):
        key = together.get(name[0], together.get(name[:2], together.get(name, name)))
        m = names.setdefault(key, len(names))
        kind = {"s": 1, "t": 3, "c": 3}.get(name[0], 0)
        made = pltpu.make_async_remote_copy(
            src_ref=src, dst_ref=dst, send_sem=send_sem.at[kind], recv_sem=recv_sem.at[m],
            device_id=target, device_id_type=pl.DeviceIdType.MESH,
        )
        return made, kind

    def send(name, ref, target):
        made, kind = copy(name, ref, ref, target)
        made.start()
        sent[kind] = sent.get(kind, 0) + ref.shape[0]

    def recv(name, ref, target):
        copy(name, ref, ref, target)[0].wait_recv()

    def pack(core, v, k, first=0, rows=PACK):
        column = (zz(k) * NY + yy(v)) * 2 + core
        return panel.at[pl.ds(pl.multiple_of(column * PACK + first, 16), rows)]

    def share(name, ref_of):
        send("s" + name, ref_of(d), sib)

    def entries(y_):
        return at_v.at[pl.ds(pl.multiple_of((z * NY + y_) * 2, 2), 2)]

    def table(z_):
        return at_v.at[pl.ds(pl.multiple_of(z_ * (2 * NY), 2), 2 * NY)]

    def chunk(part, v, k, core=None):
        return pack(d if core is None else core, v, k, *PARTS[part])

    def step_of(part, v, k):
        far = part % 2
        if (k != 0) if part < 2 else (v == 0):
            if k < 0 or (k == 4 and not far):
                return (v, k + 1 if k < 0 else -3), zp
            return (v, k - 1), zm
        if v < 0 or (v == 2 and not far):
            return (v + 1 if v < 0 else -1, k), yp
        return (v - 1, k), ym

    def name_of(part, v, k):
        return f"{part},{v},{k}"

    def send_chunk(part, v, k):
        (pv, pk), target = step_of(part, v, k)
        send(name_of(part, v, k), chunk(part, pv, pk), target)

    def arrived(part, v, k):
        share(f"{part},{v},{k}", lambda core: chunk(part, v, k, core))

    def place(n):
        return n // 32, n // 8 % 4 - 1, n % 8 - 3

    runs = []
    for n, before in zip(ORDER, (-1,) + ORDER):
        if 0 <= n < 128:
            if not 0 <= before < 128 or len(runs[-1]) == 2:
                runs.append([])
            runs[-1].append(place(n))
    for number, run in enumerate(runs):
        for one in run:
            together[name_of(*one)] = f"run{number}"

    send("t0", at_v.at[2 * c + d], sib)
    begun = 0
    for n in ORDER:
        if n < 0:
            send_chunk(*place(-1 - n))
        elif n < 128:
            if begun == len(runs) or place(n) != runs[begun][0]:
                continue
            if begun == 0:
                for part in range(4):
                    arrived(part, 0, 0)
                recv("t0", at_v.at[2 * c + e], sib)
                for name, target in (("ty+", yp), ("ty-", ym), ("ty2", y2)):
                    send(name, entries(y), target)
                own = xc.at[pl.ds(pl.multiple_of(x * PACK, BS), PACK)]
                for name, target in (("x+", xp), ("x-", xm), ("x2", x2)):
                    send("c" + name, ct_v.at[x], target)
                    send(name, own, target)
            run = runs[begun]
            begun += 1
            total = sum(PARTS[part][1] for part, _, _ in run)
            recv(name_of(*run[0]), panel.at[pl.ds(0, total)], yp)
            for one in run:
                arrived(*one)
        elif n == 128:
            recv("ty", at_v.at[pl.ds(0, 3 * 2)], yp)
            for name, target in (("tz+", zp), ("tz-", zm), ("tzz+", zpp), ("tzz-", zmm)):
                send(name, table(z), target)
        elif n == 129:
            recv("tz", at_v.at[pl.ds(0, 4 * 2 * NY)], zp)
            send("t3+", table(zz(-1)), zpp)
            send("t3-", table(zz(1)), zmm)
            send("t4", table(zz(-2)), zpp)
        else:
            recv("t3", at_v.at[pl.ds(0, 3 * 2 * NY)], zpp)
    recv("c", ct_v.at[pl.ds(0, 3)], xp)
    recv("x", xc.at[pl.ds(0, 3 * PACK)], xp)
    tables = [
        pltpu.make_async_copy(at_v, at_s, local_sem.at[0]),
        pltpu.make_async_copy(ct_v, ct_s, local_sem.at[1]),
    ]
    for made in tables:
        made.start()
    recv("s", panel.at[pl.ds(0, NC * PACK)], sib)
    for made in tables:
        made.wait()

    def block(k, i):
        return panel[pl.ds(at_s[k, 0, i] * BS, BS)]

    def tile(rows, columns):
        return jnp.concatenate(
            [jnp.concatenate([block(k, i) for k in columns], axis=1) for i in rows], axis=0
        )

    def masked(flag, values):
        return jnp.where(jnp.full(values.shape, flag, jnp.int32) != 0, values, 0.0)

    def s_ref(group_, q, half=None):
        first, rows = QS[q] * BS, QL[q] * BS
        if half is not None:
            rows //= 2
            first += half * rows
        return sb.at[pl.ds(pl.multiple_of(group_ * ROWS + first, BS), rows)]

    qrows = QR * BS
    first_q = len(names)

    def chunk_copy(group_, q, target, half=None):
        rows = qrows if half is None else qrows // 2
        first = 0 if half is None else half * rows
        ref = sb.at[pl.ds(pl.multiple_of(group_ * ROWS + q * qrows + first, BS), rows)]
        return pltpu.make_async_remote_copy(
            src_ref=ref, dst_ref=ref, send_sem=send_sem.at[2],
            recv_sem=recv_sem.at[first_q + q + (0 if half is None else QN)],
            device_id=target, device_id_type=pl.DeviceIdType.MESH,
        )

    def chunk_wait(q, forwarded):
        whole = sb.at[pl.ds(0, qrows if forwarded else 2 * qrows)]
        pltpu.make_async_remote_copy(
            src_ref=whole, dst_ref=whole, send_sem=send_sem.at[2],
            recv_sem=recv_sem.at[first_q + q + (QN if forwarded else 0)],
            device_id=xp, device_id_type=pl.DeviceIdType.MESH,
        ).wait_recv()

    kept = [ct_s[j // SLOTS, 0, j % SLOTS] for j in range(NX * SLOTS)]

    def square(q, carry):
        rows = [q * QR + i for i in range(QR)]
        total = None
        for p in range(NX * SLOTS // 2):
            term = jnp.dot(
                tile(rows, kept[2 * p : 2 * p + 2]),
                xc[pl.ds(p * 2 * BS, 2 * BS)],
                preferred_element_type=jnp.float32,
            )
            total = term if total is None else total + term
        for i, row in enumerate(rows):
            part = masked(msq[row], total[i * BS : (i + 1) * BS])
            sb[pl.ds(pl.multiple_of(x * ROWS + row * BS, BS), BS)] = part.astype(jnp.bfloat16)
        chunk_copy(x, q, xp).start()
        chunk_copy(x, q, xm).start()
        return carry

    lax.fori_loop(0, QN, square, 0)
    acc[...] = jnp.zeros_like(acc)

    def cube(group_, q):
        w = sb[pl.ds(pl.multiple_of(group_ * ROWS + q * qrows, BS), qrows)]
        columns = [group_ * RB + q * QR + k for k in range(QR)]
        acc[...] += jnp.dot(
            tile(range(RB), columns), w, preferred_element_type=jnp.float32
        )

    def own_chunk(q, carry):
        cube(x, q)
        return carry

    lax.fori_loop(0, QN, own_chunk, 0)

    def near_chunk(q, carry):
        chunk_wait(q, False)
        chunk_copy(xx(-1), q, xp, 0).start()
        chunk_copy(xx(1), q, xm, 1).start()

        def side(k, carry):
            cube(xx(2 * k - 1), q)
            return carry

        return lax.fori_loop(0, 2, side, carry)

    lax.fori_loop(0, QN, near_chunk, 0)

    def far_chunk(q, carry):
        chunk_wait(q, True)
        cube(xx(2), q)
        return carry

    lax.fori_loop(0, QN - 1, far_chunk, 0)
    sent[2] = 3 * ROWS

    for i in range(RB):
        spot = pl.ds(i * BS, BS)
        own_x = masked(mx[i], x_ref[spot].astype(jnp.float32))
        acc[spot] = 1.5 * own_x - 0.5 * acc[spot]
    chunk_wait(QN - 1, True)
    last = xx(2)
    w = sb[pl.ds(pl.multiple_of(last * ROWS + (QN - 1) * qrows, BS), qrows)]
    columns = [last * RB + (QN - 1) * QR + k for k in range(QR)]
    term = jnp.dot(tile(range(RB), columns), w, preferred_element_type=jnp.float32)
    for i in range(RB):
        spot = pl.ds(i * BS, BS)
        result = masked(mo[i], acc[spot] - 0.5 * term[i * BS : (i + 1) * BS])
        out_ref[spot] = result.astype(jnp.bfloat16)

    for kind, buffer in ((0, panel), (1, panel), (2, sb), (3, at_v)):
        if kind in sent:
            whole = buffer.at[pl.ds(0, sent[kind])]
            pltpu.make_async_remote_copy(
                src_ref=whole, dst_ref=whole, send_sem=send_sem.at[kind], recv_sem=recv_sem.at[0],
                device_id=xp, device_id_type=pl.DeviceIdType.MESH,
            ).wait_send()


def body(xmat, mask_x, mask_sq, mask_out):
    hbm = pl.BlockSpec(memory_space=pltpu.HBM)
    vmem = pl.BlockSpec(memory_space=pltpu.VMEM)
    return pl.pallas_call(
        kernel,
        out_shape=jax.ShapeDtypeStruct(xmat.shape, jnp.bfloat16),
        in_specs=[hbm] * 4,
        out_specs=vmem,
        scratch_shapes=[
            pltpu.SMEM((RB,), jnp.int32),
            pltpu.SMEM((RB,), jnp.int32),
            pltpu.SMEM((RB,), jnp.int32),
            pltpu.VMEM((ROWS, BS), jnp.bfloat16),
            pltpu.VMEM((ZERO + BS, BS), jnp.bfloat16),
            pltpu.VMEM((NX * PACK, BS), jnp.bfloat16),
            pltpu.VMEM((NX * ROWS, BS), jnp.bfloat16),
            pltpu.VMEM((ROWS, BS), jnp.float32),
            pltpu.VMEM((2 * NC + 2, 1, 128), jnp.int32),
            pltpu.VMEM((NX, 1, 128), jnp.int32),
            pltpu.SMEM((2 * NC + 2, 1, 128), jnp.int32),
            pltpu.SMEM((NX, 1, 128), jnp.int32),
            pltpu.SemaphoreType.DMA((4,)),
            pltpu.SemaphoreType.DMA((MSGS,)),
            pltpu.SemaphoreType.DMA((6,)),
        ],
        compiler_params=pltpu.CompilerParams(
            collective_id=0, has_side_effects=True, vmem_limit_bytes=53 * 1024 * 1024
        ),
    )(mask_x.reshape(RB), mask_sq.reshape(RB), mask_out.reshape(RB), xmat)


def solution(mesh):
    placed = P("row", ("col", "depth"))
    return jax.shard_map(
        body, mesh=mesh, in_specs=(placed,) * 4, out_specs=placed, check_vma=False
    )
```

```python
import jax
import jax.numpy as jnp
from jax import lax
from jax.experimental import pallas as pl
from jax.experimental.pallas import tpu as pltpu
from jax.sharding import PartitionSpec as P

BS = 128
RB = 16
SLOTS = 4
NX, NY, NZ = 4, 4, 8
NC = NY * NZ
PACK = SLOTS * BS
ZERO = 2 * NC * PACK
ROWS = RB * BS
QR = 2
QN = RB // QR
MSGS = 80

PARTS = ((0, 112), (112, 96), (208, 144), (352, 160))

ORDER = (
    -4, -52, -11, -77, -84, -100, -75, -109, -116, -43, -36, -13, -107, -68, -20, -45, 51, -60,
    -51, -53, 3, 10, -28, -3, 76, -85, -78, -69, 83, 74, -74, 99, 108, -117, -110, -101, 42, 35,
    -35, 115, -124, 12, -14, -37, 67, 19, 106, 44, -92, -19, -115, -106, -67, -99, -83, 128, 59,
    50, 52, -61, -54, 27, -27, -29, 2, -2, 84, 77, -70, -79, 68, 73, -82, -73, -66, -93, 116,
    109, -125, -111, -86, 100, 34, 13, 123, 18, -18, -50, 91, 36, 60, -62, 114, 105, 66, -105,
    -91, -114, -102, -123, 53, -55, 26, -26, 82, 98, 28, -30, -46, -21, -38, 1, -1, 81, 69, 78,
    -87, 72, -65, -80, 124, 65, -90, 17, -17, -59, -10, 110, -119, -112, -103, -118, -5, -15,
    129, 49, 92, 85, 61, 54, 104, 90, -97, -113, -71, -81, 113, 29, 25, -25, -34, -42, 45, 101,
    -47, 122, 0, 20, -22, 64, 86, 37, 79, -72, -88, -39, -63, 89, 16, 118, -24, 111, -104, -120,
    -89, -98, 58, -58, 102, 117, 4, -6, -126, -31, 9, -9, 14, 96, 112, 24, -32, -121, -127,
    -122, 46, -48, 33, -33, 70, -95, 80, 21, -23, 41, -41, -49, 130, 38, 71, -40, -96, -94, 87,
    23, 62, -64, 57, -57, 103, 119, -128, 5, -7, -56, 8, -16, -8, 88, 30, 125, 31, 47, 32, 97,
    120, 22, 40, 94, 39, 48, 126, 63, 95, 56, 121, 6, 15, 93, 55, 7, 127,
)


def kernel(mx_hbm, msq_hbm, mo_hbm, x_hbm, out_ref, mx, msq, mo, x_ref, panel, xc, sb, acc,
           at_v, ct_v, at_s, ct_s, send_sem, recv_sem, local_sem):
    x = lax.axis_index("row")
    c = lax.axis_index("col")
    d = lax.axis_index("depth")
    z, y = c // NY, c % NY
    e = 1 - d

    def yy(k):
        return (y + (k + NY)) % NY

    def zz(k):
        return (z + (k + NZ)) % NZ

    def xx(k):
        return (x + (k + NX)) % NX

    def dev(dx=0, dy=0, dz=0, core=None):
        return {
            "row": xx(dx) if dx else x,
            "col": (zz(dz) if dz else z) * NY + (yy(dy) if dy else y),
            "depth": d if core is None else core,
        }

    yp, ym, zp, zm = dev(dy=1), dev(dy=-1), dev(dz=1), dev(dz=-1)
    xp, xm, x2, sib = dev(dx=1), dev(dx=-1), dev(dx=2), dev(core=e)
    y2, zpp, zmm = dev(dy=2), dev(dz=2), dev(dz=-2)
    partners = (zp, zm, yp, ym, zpp, zmm, y2, xp, xm, x2, sib)

    barrier = pltpu.get_barrier_semaphore()
    for partner in partners:
        pl.semaphore_signal(
            barrier, inc=1, device_id=partner, device_id_type=pl.DeviceIdType.MESH
        )

    inputs = [
        pltpu.make_async_copy(src, dst, local_sem.at[2 + n])
        for n, (src, dst) in enumerate(
            ((mx_hbm, mx), (msq_hbm, msq), (mo_hbm, mo), (x_hbm, x_ref))
        )
    ]
    for made in inputs:
        made.start()
    panel[pl.ds(ZERO, BS)] = jnp.zeros((BS, BS), jnp.bfloat16)
    for made in inputs:
        made.wait()

    count = jnp.int32(0)
    index = [jnp.int32(0)] * SLOTS
    lane = lax.broadcasted_iota(jnp.int32, (1, 128), 1)
    me = 2 * c + d
    entry = jnp.full((1, 128), ZERO // BS, jnp.int32)
    for i in range(RB):
        keep = jnp.minimum(mx[i], 1)
        for s in range(SLOTS):
            here = jnp.maximum(1 - jnp.abs(count - s), 0)
            index[s] = index[s] + i * keep * here
        at = keep * (me * SLOTS + count) + (1 - keep) * (ZERO // BS)
        entry = jnp.where(lane == i, at, entry)
        count = count + keep
    column = jnp.full((1, 128), 2 * NC, jnp.int32)
    for s in range(SLOTS):
        there = jnp.minimum(jnp.maximum(count - s, 0), 1)
        k = there * (x * RB + index[s]) + (1 - there) * (2 * NC)
        column = jnp.where(lane == s, k, column)
    at_v[2 * c + d] = entry
    for core in range(2):
        at_v[2 * NC + core] = jnp.full((1, 128), ZERO // BS, jnp.int32)
    ct_v[x] = column
    for s in range(SLOTS):
        piece = x_ref[pl.ds(index[s] * BS, BS)]
        panel[pl.ds(pl.multiple_of(me * PACK + s * BS, BS), BS)] = piece
        xc[pl.ds(pl.multiple_of(x * PACK + s * BS, BS), BS)] = piece

    pl.semaphore_wait(barrier, len(partners))

    names = {}
    sent = {}
    together = {"s": "s", "x": "x", "c": "c", "ty": "ty", "tz": "tz", "t3": "t3", "t4": "t3"}

    def copy(name, src, dst, target):
        key = together.get(name[0], together.get(name[:2], together.get(name, name)))
        m = names.setdefault(key, len(names))
        kind = {"s": 1, "t": 3, "c": 3}.get(name[0], 0)
        made = pltpu.make_async_remote_copy(
            src_ref=src, dst_ref=dst, send_sem=send_sem.at[kind], recv_sem=recv_sem.at[m],
            device_id=target, device_id_type=pl.DeviceIdType.MESH,
        )
        return made, kind

    def send(name, ref, target):
        made, kind = copy(name, ref, ref, target)
        made.start()
        sent[kind] = sent.get(kind, 0) + ref.shape[0]

    def recv(name, ref, target):
        copy(name, ref, ref, target)[0].wait_recv()

    def pack(core, v, k, first=0, rows=PACK):
        column = (zz(k) * NY + yy(v)) * 2 + core
        return panel.at[pl.ds(pl.multiple_of(column * PACK + first, 16), rows)]

    def share(name, ref_of):
        send("s" + name, ref_of(d), sib)

    def entries(y_):
        return at_v.at[pl.ds(pl.multiple_of((z * NY + y_) * 2, 2), 2)]

    def table(z_):
        return at_v.at[pl.ds(pl.multiple_of(z_ * (2 * NY), 2), 2 * NY)]

    def chunk(part, v, k, core=None):
        return pack(d if core is None else core, v, k, *PARTS[part])

    def step_of(part, v, k):
        far = part % 2
        if (k != 0) if part < 2 else (v == 0):
            if k < 0 or (k == 4 and not far):
                return (v, k + 1 if k < 0 else -3), zp
            return (v, k - 1), zm
        if v < 0 or (v == 2 and not far):
            return (v + 1 if v < 0 else -1, k), yp
        return (v - 1, k), ym

    def name_of(part, v, k):
        return f"{part},{v},{k}"

    def send_chunk(part, v, k):
        (pv, pk), target = step_of(part, v, k)
        send(name_of(part, v, k), chunk(part, pv, pk), target)

    def arrived(part, v, k):
        share(f"{part},{v},{k}", lambda core: chunk(part, v, k, core))

    def place(n):
        return n // 32, n // 8 % 4 - 1, n % 8 - 3

    runs = []
    for n, before in zip(ORDER, (-1,) + ORDER):
        if 0 <= n < 128:
            if not 0 <= before < 128 or len(runs[-1]) == 4:
                runs.append([])
            runs[-1].append(place(n))
    for number, run in enumerate(runs):
        for one in run:
            together[name_of(*one)] = f"run{number}"

    send("t0", at_v.at[2 * c + d], sib)
    begun = 0
    for n in ORDER:
        if n < 0:
            send_chunk(*place(-1 - n))
        elif n < 128:
            if begun == len(runs) or place(n) != runs[begun][0]:
                continue
            if begun == 0:
                for part in range(4):
                    arrived(part, 0, 0)
                recv("t0", at_v.at[2 * c + e], sib)
                for name, target in (("ty+", yp), ("ty-", ym), ("ty2", y2)):
                    send(name, entries(y), target)
                own = xc.at[pl.ds(pl.multiple_of(x * PACK, BS), PACK)]
                for name, target in (("x+", xp), ("x-", xm), ("x2", x2)):
                    send("c" + name, ct_v.at[x], target)
                    send(name, own, target)
            run = runs[begun]
            begun += 1
            total = sum(PARTS[part][1] for part, _, _ in run)
            recv(name_of(*run[0]), panel.at[pl.ds(0, total)], yp)
            for one in run:
                arrived(*one)
        elif n == 128:
            recv("ty", at_v.at[pl.ds(0, 3 * 2)], yp)
            for name, target in (("tz+", zp), ("tz-", zm), ("tzz+", zpp), ("tzz-", zmm)):
                send(name, table(z), target)
        elif n == 129:
            recv("tz", at_v.at[pl.ds(0, 4 * 2 * NY)], zp)
            send("t3+", table(zz(-1)), zpp)
            send("t3-", table(zz(1)), zmm)
            send("t4", table(zz(-2)), zpp)
        else:
            recv("t3", at_v.at[pl.ds(0, 3 * 2 * NY)], zpp)
    recv("c", ct_v.at[pl.ds(0, 3)], xp)
    recv("x", xc.at[pl.ds(0, 3 * PACK)], xp)
    tables = [
        pltpu.make_async_copy(at_v, at_s, local_sem.at[0]),
        pltpu.make_async_copy(ct_v, ct_s, local_sem.at[1]),
    ]
    for made in tables:
        made.start()
    recv("s", panel.at[pl.ds(0, NC * PACK)], sib)
    for made in tables:
        made.wait()

    def block(k, i):
        return panel[pl.ds(at_s[k, 0, i] * BS, BS)]

    def tile(rows, columns):
        return jnp.concatenate(
            [jnp.concatenate([block(k, i) for k in columns], axis=1) for i in rows], axis=0
        )

    def masked(flag, values):
        return jnp.where(jnp.full(values.shape, flag, jnp.int32) != 0, values, 0.0)

    def s_ref(group_, q, half=None):
        first, rows = QS[q] * BS, QL[q] * BS
        if half is not None:
            rows //= 2
            first += half * rows
        return sb.at[pl.ds(pl.multiple_of(group_ * ROWS + first, BS), rows)]

    qrows = QR * BS
    first_q = len(names)

    def chunk_copy(group_, q, target, half=None):
        rows = qrows if half is None else qrows // 2
        first = 0 if half is None else half * rows
        ref = sb.at[pl.ds(pl.multiple_of(group_ * ROWS + q * qrows + first, BS), rows)]
        return pltpu.make_async_remote_copy(
            src_ref=ref, dst_ref=ref, send_sem=send_sem.at[2],
            recv_sem=recv_sem.at[first_q + q + (0 if half is None else QN)],
            device_id=target, device_id_type=pl.DeviceIdType.MESH,
        )

    def chunk_wait(q, forwarded):
        whole = sb.at[pl.ds(0, qrows if forwarded else 2 * qrows)]
        pltpu.make_async_remote_copy(
            src_ref=whole, dst_ref=whole, send_sem=send_sem.at[2],
            recv_sem=recv_sem.at[first_q + q + (QN if forwarded else 0)],
            device_id=xp, device_id_type=pl.DeviceIdType.MESH,
        ).wait_recv()

    kept = [ct_s[j // SLOTS, 0, j % SLOTS] for j in range(NX * SLOTS)]

    def square(q, carry):
        rows = [q * QR + i for i in range(QR)]
        total = None
        for p in range(NX * SLOTS // 2):
            term = jnp.dot(
                tile(rows, kept[2 * p : 2 * p + 2]),
                xc[pl.ds(p * 2 * BS, 2 * BS)],
                preferred_element_type=jnp.float32,
            )
            total = term if total is None else total + term
        for i, row in enumerate(rows):
            part = masked(msq[row], total[i * BS : (i + 1) * BS])
            sb[pl.ds(pl.multiple_of(x * ROWS + row * BS, BS), BS)] = part.astype(jnp.bfloat16)
        chunk_copy(x, q, xp).start()
        chunk_copy(x, q, xm).start()
        return carry

    lax.fori_loop(0, QN, square, 0)
    acc[...] = jnp.zeros_like(acc)

    def cube(group_, q):
        w = sb[pl.ds(pl.multiple_of(group_ * ROWS + q * qrows, BS), qrows)]
        columns = [group_ * RB + q * QR + k for k in range(QR)]
        acc[...] += jnp.dot(
            tile(range(RB), columns), w, preferred_element_type=jnp.float32
        )

    def own_chunk(q, carry):
        cube(x, q)
        return carry

    lax.fori_loop(0, QN, own_chunk, 0)

    def near_chunk(q, carry):
        chunk_wait(q, False)
        chunk_copy(xx(-1), q, xp, 0).start()
        chunk_copy(xx(1), q, xm, 1).start()

        def side(k, carry):
            cube(xx(2 * k - 1), q)
            return carry

        return lax.fori_loop(0, 2, side, carry)

    lax.fori_loop(0, QN, near_chunk, 0)

    def far_chunk(q, carry):
        chunk_wait(q, True)
        cube(xx(2), q)
        return carry

    lax.fori_loop(0, QN - 1, far_chunk, 0)
    sent[2] = 3 * ROWS

    for i in range(RB):
        spot = pl.ds(i * BS, BS)
        own_x = masked(mx[i], x_ref[spot].astype(jnp.float32))
        acc[spot] = 1.5 * own_x - 0.5 * acc[spot]
    chunk_wait(QN - 1, True)
    last = xx(2)
    w = sb[pl.ds(pl.multiple_of(last * ROWS + (QN - 1) * qrows, BS), qrows)]
    columns = [last * RB + (QN - 1) * QR + k for k in range(QR)]
    term = jnp.dot(tile(range(RB), columns), w, preferred_element_type=jnp.float32)
    for i in range(RB):
        spot = pl.ds(i * BS, BS)
        result = masked(mo[i], acc[spot] - 0.5 * term[i * BS : (i + 1) * BS])
        out_ref[spot] = result.astype(jnp.bfloat16)

    for kind, buffer in ((0, panel), (1, panel), (2, sb), (3, at_v)):
        if kind in sent:
            whole = buffer.at[pl.ds(0, sent[kind])]
            pltpu.make_async_remote_copy(
                src_ref=whole, dst_ref=whole, send_sem=send_sem.at[kind], recv_sem=recv_sem.at[0],
                device_id=xp, device_id_type=pl.DeviceIdType.MESH,
            ).wait_send()


def body(xmat, mask_x, mask_sq, mask_out):
    hbm = pl.BlockSpec(memory_space=pltpu.HBM)
    vmem = pl.BlockSpec(memory_space=pltpu.VMEM)
    return pl.pallas_call(
        kernel,
        out_shape=jax.ShapeDtypeStruct(xmat.shape, jnp.bfloat16),
        in_specs=[hbm] * 4,
        out_specs=vmem,
        scratch_shapes=[
            pltpu.SMEM((RB,), jnp.int32),
            pltpu.SMEM((RB,), jnp.int32),
            pltpu.SMEM((RB,), jnp.int32),
            pltpu.VMEM((ROWS, BS), jnp.bfloat16),
            pltpu.VMEM((ZERO + BS, BS), jnp.bfloat16),
            pltpu.VMEM((NX * PACK, BS), jnp.bfloat16),
            pltpu.VMEM((NX * ROWS, BS), jnp.bfloat16),
            pltpu.VMEM((ROWS, BS), jnp.float32),
            pltpu.VMEM((2 * NC + 2, 1, 128), jnp.int32),
            pltpu.VMEM((NX, 1, 128), jnp.int32),
            pltpu.SMEM((2 * NC + 2, 1, 128), jnp.int32),
            pltpu.SMEM((NX, 1, 128), jnp.int32),
            pltpu.SemaphoreType.DMA((4,)),
            pltpu.SemaphoreType.DMA((MSGS,)),
            pltpu.SemaphoreType.DMA((6,)),
        ],
        compiler_params=pltpu.CompilerParams(
            collective_id=0, has_side_effects=True, vmem_limit_bytes=53 * 1024 * 1024
        ),
    )(mask_x.reshape(RB), mask_sq.reshape(RB), mask_out.reshape(RB), xmat)


def solution(mesh):
    placed = P("row", ("col", "depth"))
    return jax.shard_map(
        body, mesh=mesh, in_specs=(placed,) * 4, out_specs=placed, check_vma=False
    )
```
